512 devices in a mesh: row: 16 (over z_lo, x), col: 32 (over z_hi, y, core).
Axes of the slice: x: 4, y: 4, z: 16 (z_hi: 4, z_lo: 4; z = z_hi * 4 + z_lo), core: 2. Of those that a mesh axis runs over, the one named last changes fastest.
Arguments:
- features: bfloat16 [65536, 256], P(('row', 'col')), may hold values from -6 to 6
- adj_tiles: bfloat16 [16, 32, 96, 128, 128], P('row', 'col'), may hold values from -0.109375 to 0.109375
- tile_row: int32 [16, 32, 96], P('row', 'col'), may hold values from 0 to 31, as said below
- tile_col: int32 [16, 32, 96], P('row', 'col'), may hold values from 0 to 15
- tile_count: int32 [16, 32], P('row', 'col'), may hold values from 8 to 96, as said below
- w_self: bfloat16 [256, 256], replicated, may hold values from -0.375 to 0.375
- w_neigh: bfloat16 [256, 256], replicated, may hold values from -0.375 to 0.375
- bias_vec: float32 [256], replicated, may hold values from -3 to 3
- cotangent: bfloat16 [65536, 256], P(('row', 'col')), may hold values from -6 to 6
Outputs:
- layer_out: bfloat16 [65536, 256], P(('row', 'col'))
- grad_features: bfloat16 [65536, 256], P(('row', 'col'))
- grad_self: float32 [256, 256], replicated
- grad_neigh: float32 [256, 256], replicated
- grad_bias: float32 [256], replicated
The draws below stay inside these ranges and needn't reach their ends.
Inputs may be any that keep to these rules, and one draw needn't show every extreme that they name: Within each block the 96 (tile_row, tile_col) pairs are distinct. `tile_count`: some block has all 96 slots occupied.
All inputs are finite; a program needn't handle non-finite values.
Results may differ from the reference program's by a relative error of at most 0.022.
Values may be sent and summed in bfloat16 or wider, within the bound.
A program may use at most 128 MiB of HBM per device.

```python
import jax
import jax.numpy as jnp
from jax import lax

F = 256
TILE = 128
B = 128
NODES = 65536
ROWBLK = 4096
COLBLK = 2048
TROWS = 32
TCOLS = 16
TMAX = 96
N_ROW = 16
N_COL = 32


def block_slots(key):
    keys = jax.random.split(key, N_ROW * N_COL)
    slots = jax.vmap(lambda sub: jax.random.permutation(sub, TROWS * TCOLS)[:TMAX])(keys)
    return slots.reshape(N_ROW, N_COL, TMAX).astype(jnp.int32)


def draw_tile_row(key, part):
    slots = block_slots(key)
    return (slots // TCOLS).astype(jnp.int32)


def draw_tile_col(key, part):
    slots = block_slots(key)
    return (slots % TCOLS).astype(jnp.int32)


def draw_tile_count(key, part):
    key = jax.random.fold_in(key, 7)
    row_ids = jnp.arange(N_ROW, dtype=jnp.int32)[:, None]
    col_ids = jnp.arange(N_COL, dtype=jnp.int32)[None, :]
    stride = max(1, N_COL // N_ROW)
    nearby = (col_ids - row_ids * stride) % N_COL < 2
    near_counts = jax.random.randint(jax.random.fold_in(key, 1), (N_ROW, N_COL), max(1, 2 * TMAX // 3), TMAX + 1)
    far_counts = jax.random.randint(jax.random.fold_in(key, 2), (N_ROW, N_COL), max(1, TMAX // 12), max(2, TMAX // 4 + 1))
    counts = jnp.where(nearby, near_counts, far_counts).astype(jnp.int32)
    fullest = jax.random.randint(jax.random.fold_in(key, 3), (), 0, N_ROW)
    counts = counts.at[fullest, fullest * stride % N_COL].set(TMAX)
    return counts.astype(jnp.int32)


def shard_levels(own_key, dims, pieces, smallest, top_value):
    level = 1.0
    for position, parts in pieces:
        steps = jax.random.uniform(jax.random.fold_in(jax.random.fold_in(own_key, 6), position), (parts,), jnp.float32, smallest / len(pieces), top_value / len(pieces))
        level = level * jnp.repeat(jnp.exp(steps), dims[position] // parts).reshape((-1,) + (1,) * (len(dims) - 1 - position))
    return level


def gaussian(rng, shape, deviation, most, shards=(), kind=jnp.bfloat16):
    loudness = shard_levels(rng, shape, shards, -0.22, 0.18) if shards else 1.0
    array = jax.random.normal(rng, shape, jnp.float32) * deviation * loudness
    return jnp.minimum(jnp.maximum(array, -most), most).astype(kind)


def setup_inputs(seed: int = 0) -> dict:
    splits = jax.random.split(jax.random.key(seed), 10)
    return {
        "features": gaussian(splits[0], (NODES, F), 1.0, 6.0, ((0, 512),)),
        "adj_tiles": gaussian(splits[1], (N_ROW, N_COL, TMAX, TILE, TILE), (TMAX * TILE * TILE // (4 * B)) ** -0.5, 0.109375, ((0, 16), (1, 32))),
        "tile_row": draw_tile_row(jax.random.fold_in(splits[9], 71), 0),
        "tile_col": draw_tile_col(jax.random.fold_in(splits[9], 71), 0),
        "tile_count": draw_tile_count(jax.random.fold_in(splits[9], 71), 0),
        "w_self": gaussian(splits[5], (F, F), F ** -0.5, 0.375),
        "w_neigh": gaussian(splits[6], (F, F), F ** -0.5, 0.375),
        "bias_vec": gaussian(splits[7], (F,), 0.5, 3.0, (), jnp.float32),
        "cotangent": gaussian(splits[8], (NODES, F), 1.0, 6.0, ((0, 512),)),
    }


def reference(features, adj_tiles, tile_row, tile_col, tile_count, w_self, w_neigh, bias_vec, cotangent):
    feat_grid = features.reshape(N_ROW, N_COL, B, F)
    slot_ids = jnp.arange(TMAX)

    def forward_block(row_index, col_index):
        column_block = feat_grid[:, col_index].reshape(TCOLS, TILE, F).astype(jnp.float32)
        picked = column_block[tile_col[row_index, col_index]]
        masked = (slot_ids < tile_count[row_index, col_index]).astype(jnp.float32)
        values = adj_tiles[row_index, col_index].astype(jnp.float32)
        product = jnp.einsum('tab,tbf->taf', values, picked) * masked[:, None, None]
        summed = jnp.zeros((TROWS, TILE, F), jnp.float32).at[tile_row[row_index, col_index]].add(product)
        rounded = lax.optimization_barrier(summed.astype(jnp.bfloat16))
        return rounded.astype(jnp.float32).reshape(ROWBLK, F)

    def row_sum(row_index):

        def step(carry, col_index):
            return (carry + forward_block(row_index, col_index), None)
        total, _ = lax.scan(step, jnp.zeros((ROWBLK, F), jnp.float32), jnp.arange(N_COL))
        return total
    aggregate = lax.map(row_sum, jnp.arange(N_ROW)).reshape(NODES, F).astype(jnp.bfloat16)
    preact = jnp.dot(features, w_self, preferred_element_type=jnp.float32) + jnp.dot(aggregate, w_neigh, preferred_element_type=jnp.float32) + bias_vec
    sigma = jax.nn.sigmoid(preact)
    layer_out = (preact * sigma).astype(jnp.bfloat16)
    grad_pre = cotangent.astype(jnp.float32) * sigma * (1.0 + preact * (1.0 - sigma))
    grad_pre_b = grad_pre.astype(jnp.bfloat16)
    neigh_grad = jnp.dot(grad_pre_b, w_neigh.T, preferred_element_type=jnp.float32).astype(jnp.bfloat16)
    grad_rows = neigh_grad.reshape(N_ROW, TROWS, TILE, F)

    def backward_block(row_index, col_index):
        picked = grad_rows[row_index][tile_row[row_index, col_index]].astype(jnp.float32)
        masked = (slot_ids < tile_count[row_index, col_index]).astype(jnp.float32)
        values = adj_tiles[row_index, col_index].astype(jnp.float32)
        product = jnp.einsum('tab,taf->tbf', values, picked) * masked[:, None, None]
        summed = jnp.zeros((TCOLS, TILE, F), jnp.float32).at[tile_col[row_index, col_index]].add(product)
        rounded = lax.optimization_barrier(summed.astype(jnp.bfloat16))
        return rounded.astype(jnp.float32).reshape(COLBLK, F)

    def col_sum(col_index):

        def step(carry, row_index):
            return (carry + backward_block(row_index, col_index), None)
        total, _ = lax.scan(step, jnp.zeros((COLBLK, F), jnp.float32), jnp.arange(N_ROW))
        return total
    back_cols = lax.map(col_sum, jnp.arange(N_COL)).reshape(N_COL, N_ROW, B, F)
    back_nodes = jnp.transpose(back_cols, (1, 0, 2, 3)).reshape(NODES, F)
    grad_features = (jnp.dot(grad_pre_b, w_self.T, preferred_element_type=jnp.float32) + back_nodes).astype(jnp.bfloat16)
    factor = 1.0 / jnp.sqrt(jnp.float32(NODES))
    grad_self = jnp.dot(features.T, grad_pre_b, preferred_element_type=jnp.float32) * factor
    grad_neigh = jnp.dot(aggregate.T, grad_pre_b, preferred_element_type=jnp.float32) * factor
    grad_bias = lax.optimization_barrier(jnp.sum(grad_pre, axis=0)) * factor
    return (layer_out, grad_features, grad_self, grad_neigh, grad_bias)
```

```python
import jax
import jax.numpy as jnp
from jax import lax
from jax.experimental import pallas as pl
from jax.experimental.pallas import tpu as pltpu
from jax.sharding import PartitionSpec as P

MESH = pl.DeviceIdType.MESH
BF = jnp.bfloat16
F32 = jnp.float32
SLOTS = 96
ZERO = SLOTS
TN = (((0,), (0,)), ((), ()))
NT = (((1,), (1,)), ((), ()))
Z_FAR = (2, 1, 3, 0)
Z_NEAR = (0, 1, 3, 2)
RING = (1, 3, 2)


def mod4(v):
    return lax.rem(v, 4)


def dot(a, b):
    return jnp.dot(a, b, preferred_element_type=F32)


def kernel(
    inv, feat, tiles, w_self, w_neigh, bias, cot,
    out, gfeat, gself, gneigh, gbias,
    A, T, X, PA, CR, Y, YR, ZS, ZR, G, ACC, BP, XR, XS, LR,
    W, M, MC, M1, MX, M2, MY, M3, ML, M4, MH, R,
    tsem, s1z, r1z, s1x, r1x, s3c, r3c, s3y, r3y, s3z, r3z,
    s5z, r5z, s5y, r5y, s5c, r5c, s6x, r6x, s6l, r6l, sw, rw,
):
    i = lax.axis_index("row")
    j = lax.axis_index("col")
    zl, x = lax.div(i, 4), lax.rem(i, 4)
    zh, yc = lax.div(j, 8), lax.rem(j, 8)
    y, c = lax.div(yc, 2), lax.rem(yc, 2)
    oc = 1 - c

    def partner(d):
        if d == 0:
            return zl
        if d == 1:
            return zl + 1 - 2 * lax.rem(zl, 2)
        if d == 2:
            return mod4(zl + 2)
        return 3 - zl

    def dev(zl_=zl, x_=x, zh_=zh, y_=y, c_=c):
        return (zl_ * 4 + x_, zh_ * 8 + y_ * 2 + c_)

    sent = []

    def send(src, dst, ssem, rsem, device):
        copy = pltpu.make_async_remote_copy(
            src_ref=src, dst_ref=dst, send_sem=ssem, recv_sem=rsem, device_id=device, device_id_type=MESH
        )
        copy.start()
        sent.append(copy)
        return copy

    load = pltpu.make_async_copy(tiles.at[0, 0], T.at[pl.ds(0, SLOTS)], tsem)
    load.start()

    barrier = pltpu.get_barrier_semaphore()
    peers = [dev(c_=oc)]
    for d in (1, 2, 3):
        peers += [dev(zl_=partner(d)), dev(x_=mod4(x + d)), dev(y_=mod4(y + d)), dev(zh_=mod4(zh + d))]
    for peer in peers:
        pl.semaphore_signal(barrier, inc=1, device_id=peer, device_id_type=MESH)
    pl.semaphore_wait(barrier, len(peers))

    z_in = {d: send(feat, X.at[i], s1z.at[d - 1], r1z.at[d - 1], dev(zl_=partner(d))) for d in (1, 2, 3)}
    x_in = []
    for d in RING:
        x_in.append(send(feat, X.at[i], s1x.at[0, d - 1], r1x.at[0, d - 1], dev(x_=mod4(x + d))))
    X[i] = feat[...]
    T[ZERO] = jnp.zeros((128, 128), BF)
    load.wait()

    def densify(first, count):
        @pl.loop(first, first + count)
        def _(p):
            rows = pl.ds(pl.multiple_of(p * 128, 128), 128)
            for q in range(16):
                A[rows, q * 128 : (q + 1) * 128] = T[inv[p * 16 + q]]

    densify(0, 11)
    for d in (1, 2, 3):
        z_in[d].wait_recv()
        block = X.at[partner(d) * 4 + x]
        for e in RING:
            x_in.append(send(block, block, s1x.at[d, e - 1], r1x.at[d, e - 1], dev(x_=mod4(x + e))))
        densify(4 + 7 * d, 7)
    own_term = dot(feat[...], w_self[...]) + bias[...]
    for copy in x_in:
        copy.wait_recv()

    core_in, y_in, zr_in = {}, {}, {}

    def after_core(n):
        zq = mod4(zh + Z_FAR[n])
        core_in[n].wait_recv()
        Y[zq] = (PA[zq, c].astype(F32) + CR[n].astype(F32)).astype(BF)
        y_in[n] = [
            send(Y.at[zq, mod4(y + d)], YR.at[n, d - 1], s3y.at[n, d - 1], r3y.at[n, d - 1], dev(y_=mod4(y + d)))
            for d in RING
        ]

    for n in range(4):
        zq = mod4(zh + Z_FAR[n])
        rows = pl.ds(pl.multiple_of(zq * 1024, 1024), 1024)
        PA[zq] = dot(A[rows, :], X[...].reshape(2048, 256)).astype(BF).reshape(2, 4, 128, 256)
        core_in[n] = send(PA.at[zq, oc], CR.at[n], s3c.at[n], r3c.at[n], dev(c_=oc))
        if n:
            after_core(n - 1)
    after_core(3)
    for n in range(4):
        zq = mod4(zh + Z_FAR[n])
        for copy in y_in[n]:
            copy.wait_recv()
        total = Y[zq, y].astype(F32)
        for d in range(3):
            total = total + YR[n, d].astype(F32)
        if n < 3:
            ZS[n] = total.astype(BF)
            dz = Z_FAR[n]
            zr_in[dz] = send(ZS.at[n], ZR.at[dz - 1], s3z.at[dz - 1], r3z.at[dz - 1], dev(zh_=mod4(zh + dz)))
    for dz in RING:
        zr_in[dz].wait_recv()
        total = total + ZR[dz - 1].astype(F32)
    aggregate = total.astype(BF)

    preact = own_term + dot(aggregate, w_neigh[...])
    sigma = jax.nn.sigmoid(preact)
    out[...] = (preact * sigma).astype(BF)
    grad_pre = cot[...].astype(F32) * sigma * (1.0 + preact * (1.0 - sigma))
    grad_pre_b = grad_pre.astype(BF)
    G[zh, c, y] = lax.dot_general(grad_pre_b, w_neigh[...], NT, preferred_element_type=F32).astype(BF)

    own = G.at[zh, c, y]
    gz_in = {dz: send(own, own, s5z.at[dz - 1], r5z.at[dz - 1], dev(zh_=mod4(zh + dz))) for dz in (2, 1, 3)}
    gy_in, gc_in = {}, {}

    def send_y(dz):
        block = G.at[mod4(zh + 4 - dz), c, y]
        gy_in[dz] = [
            send(block, block, s5y.at[dz, d - 1], r5y.at[dz, d - 1], dev(y_=mod4(y + d))) for d in RING
        ]

    def send_core(dz):
        for copy in gy_in[dz]:
            copy.wait_recv()
        slab = G.at[mod4(zh + 4 - dz), c]
        gc_in[dz] = send(slab, slab, s5c.at[dz], r5c.at[dz], dev(c_=oc))

    def back(dz, part):
        zq = mod4(zh + 4 - dz)
        rows = pl.ds(pl.multiple_of(zq * 1024, 1024), 1024)
        columns = pl.ds(pl.multiple_of(part * 512, 512), 512)
        return lax.dot_general(A[rows, columns], G[zq].reshape(1024, 256), TN, preferred_element_type=F32)

    def back_all(dz, first):
        gc_in[dz].wait_recv()

        @pl.loop(0, 4)
        def _(part):
            if first:
                ACC[part] = back(dz, part)
            else:
                ACC[part] += back(dz, part)

    send_y(0)

    W[0:256] = lax.dot_general(feat[...], grad_pre_b, TN, preferred_element_type=F32)
    W[256:512] = lax.dot_general(aggregate, grad_pre_b, TN, preferred_element_type=F32)
    ones = jnp.sum(grad_pre, axis=0, keepdims=True)
    row_id = lax.broadcasted_iota(jnp.int32, (8, 128), 0)
    bias_tile = jnp.where(row_id == 0, ones[:, :128], jnp.where(row_id == 1, ones[:, 128:], 0.0))
    gpw = lax.dot_general(grad_pre_b, w_self[...], NT, preferred_element_type=F32)

    @pl.loop(0, 32)
    def _(q):
        rows = W[pl.ds(pl.multiple_of(q * 16, 16), 16), :]
        a, b = lax.div(q, 16), lax.rem(q, 16)
        u, v = lax.div(b, 4), lax.rem(b, 4)
        M[a, u, v, 0] = rows[0:8, 0:128]
        M[a, u, v, 1] = rows[0:8, 128:256]
        M[a, u, v, 2] = rows[8:16, 0:128]
        M[a, u, v, 3] = rows[8:16, 128:256]
        M[a, u, v, 4] = bias_tile

    wc = send(M.at[oc], MC, sw.at[0], rw.at[0], dev(c_=oc))
    wc.wait_recv()
    M1[...] = M[c] + MC[...]
    wx = [send(M1.at[mod4(x + d)], MX.at[d - 1], sw.at[d], rw.at[d], dev(x_=mod4(x + d))) for d in RING]

    gz_in[1].wait_recv()
    send_y(1)
    gz_in[3].wait_recv()
    send_y(3)
    send_core(0)
    for copy in wx:
        copy.wait_recv()
    M2[...] = M1[x] + MX[0] + MX[1] + MX[2]
    wy = [send(M2.at[mod4(y + d)], MY.at[d - 1], sw.at[3 + d], rw.at[3 + d], dev(y_=mod4(y + d))) for d in RING]
    gz_in[2].wait_recv()
    send_y(2)
    back_all(0, True)
    send_core(1)
    for copy in wy:
        copy.wait_recv()
    M3[...] = M2[y] + MY[0] + MY[1] + MY[2]
    wl = [send(M3, ML.at[d - 1], sw.at[6 + d], rw.at[6 + d], dev(zl_=partner(d))) for d in (1, 2, 3)]
    send_core(3)
    back_all(1, False)
    for copy in wl:
        copy.wait_recv()
    M4[...] = M3[...] + ML[0] + ML[1] + ML[2]
    wh = [send(M4, MH.at[d - 1], sw.at[9 + d], rw.at[9 + d], dev(zh_=mod4(zh + d))) for d in (2, 1, 3)]
    back_all(3, False)
    send_core(2)
    gc_in[2].wait_recv()

    x6, l6 = [], {}
    for n in range(4):
        part = partner(3 - n)
        BP[part] = (ACC[part] + back(2, part)).astype(BF).reshape(4, 128, 256)
        x6.append([
            send(BP.at[part, mod4(x + d)], XR.at[n, d - 1], s6x.at[n, d - 1], r6x.at[n, d - 1], dev(x_=mod4(x + d)))
            for d in RING
        ])

    def after_x(n):
        d = 3 - n
        part = partner(d)
        for copy in x6[n]:
            copy.wait_recv()
        total = BP[part, x].astype(F32)
        for e in range(3):
            total = total + XR[n, e].astype(F32)
        if d:
            XS[n] = total.astype(BF)
            l6[d] = send(XS.at[n], LR.at[d - 1], s6l.at[d - 1], r6l.at[d - 1], dev(zl_=partner(d)))
        return total

    for copy in wh:
        copy.wait_recv()
    sums = M4[...] + (MH[0] + MH[1] + MH[2])
    R[c, x, y] = sums[0:4]
    block = R.at[c, x, y]
    vy = [send(block, block, sw.at[12 + d], rw.at[12 + d], dev(y_=mod4(y + d))) for d in RING]
    after_x(0)
    after_x(1)
    for copy in vy:
        copy.wait_recv()
    slab = R.at[c, x]
    vx = [send(slab, slab, sw.at[15 + d], rw.at[15 + d], dev(x_=mod4(x + d))) for d in RING]
    after_x(2)
    total = after_x(3)
    for copy in vx:
        copy.wait_recv()
    half = R.at[c]
    vc = send(half, half, sw.at[19], rw.at[19], dev(c_=oc))
    for d in (1, 2, 3):
        l6[d].wait_recv()
        total = total + LR[d - 1].astype(F32)
    gfeat[...] = (total + gpw).astype(BF)
    factor = 1.0 / 256.0
    gbias[...] = sums[4] * factor
    vc.wait_recv()

    @pl.loop(0, 16)
    def _(q):
        rows = pl.ds(pl.multiple_of(q * 16, 16), 16)
        u, v = lax.div(q, 4), lax.rem(q, 4)
        for a, ref in ((0, gself), (1, gneigh)):
            upper = jnp.concatenate([R[a, u, v, 0], R[a, u, v, 1]], axis=1)
            lower = jnp.concatenate([R[a, u, v, 2], R[a, u, v, 3]], axis=1)
            ref[rows, :] = jnp.concatenate([upper, lower], axis=0) * factor

    for copy in sent:
        copy.wait_send()


def body(features, adj_tiles, tile_row, tile_col, tile_count, w_self, w_neigh, bias_vec, cotangent):
    rows, cols = tile_row[0, 0], tile_col[0, 0]
    placed = (rows // 8) * 8 + (rows % 2) * 4 + (rows % 8) // 2
    where = placed * 16 + cols
    slot = jnp.arange(SLOTS, dtype=jnp.int32)
    hit = (where[:, None] == jnp.arange(512, dtype=jnp.int32)[None, :]) & (slot < tile_count[0, 0])[:, None]
    inv = jnp.min(jnp.where(hit, slot[:, None], ZERO), axis=0)
    vmem = pl.BlockSpec(memory_space=pltpu.VMEM)
    dma = pltpu.SemaphoreType.DMA
    sds = jax.ShapeDtypeStruct
    out, gfeat, gself, gneigh, gbias = pl.pallas_call(
        kernel,
        out_shape=(
            sds((128, 256), BF), sds((128, 256), BF), sds((256, 256), F32), sds((256, 256), F32), sds((8, 128), F32),
        ),
        in_specs=[
            pl.BlockSpec(memory_space=pltpu.SMEM), vmem, pl.BlockSpec(memory_space=pl.ANY), vmem, vmem, vmem, vmem,
        ],
        out_specs=(vmem,) * 5,
        scratch_shapes=[
            pltpu.VMEM((4096, 2048), BF),
            pltpu.VMEM((SLOTS + 1, 128, 128), BF),
            pltpu.VMEM((16, 128, 256), BF),
            pltpu.VMEM((4, 2, 4, 128, 256), BF),
            pltpu.VMEM((4, 4, 128, 256), BF),
            pltpu.VMEM((4, 4, 128, 256), BF),
            pltpu.VMEM((4, 3, 128, 256), BF),
            pltpu.VMEM((3, 128, 256), BF),
            pltpu.VMEM((3, 128, 256), BF),
            pltpu.VMEM((4, 2, 4, 128, 256), BF),
            pltpu.VMEM((4, 512, 256), F32),
            pltpu.VMEM((4, 4, 128, 256), BF),
            pltpu.VMEM((4, 3, 128, 256), BF),
            pltpu.VMEM((3, 128, 256), BF),
            pltpu.VMEM((3, 128, 256), BF),
            pltpu.VMEM((512, 256), F32),
            pltpu.VMEM((2, 4, 4, 5, 8, 128), F32),
            pltpu.VMEM((4, 4, 5, 8, 128), F32),
            pltpu.VMEM((4, 4, 5, 8, 128), F32),
            pltpu.VMEM((3, 4, 5, 8, 128), F32),
            pltpu.VMEM((4, 5, 8, 128), F32),
            pltpu.VMEM((3, 5, 8, 128), F32),
            pltpu.VMEM((5, 8, 128), F32),
            pltpu.VMEM((3, 5, 8, 128), F32),
            pltpu.VMEM((5, 8, 128), F32),
            pltpu.VMEM((3, 5, 8, 128), F32),
            pltpu.VMEM((2, 4, 4, 4, 8, 128), F32),
            dma,
            dma((3,)), dma((3,)), dma((4, 3)), dma((4, 3)),
            dma((4,)), dma((4,)), dma((4, 3)), dma((4, 3)), dma((3,)), dma((3,)),
            dma((3,)), dma((3,)), dma((4, 3)), dma((4, 3)), dma((4,)), dma((4,)),
            dma((4, 3)), dma((4, 3)), dma((3,)), dma((3,)),
            dma((20,)), dma((20,)),
        ],
        compiler_params=pltpu.CompilerParams(
            collective_id=0, has_side_effects=True, vmem_limit_bytes=56 * 2**20
        ),
    )(inv, features, adj_tiles, w_self, w_neigh, bias_vec.reshape(1, 256), cotangent)
    return out, gfeat, gself, gneigh, gbias[0:2].reshape(256)


def solution(mesh):
    placed = (
        P(("row", "col"), None),
        P("row", "col", None, None, None),
        P("row", "col", None),
        P("row", "col", None),
        P("row", "col"),
        P(),
        P(),
        P(),
        P(("row", "col"), None),
    )
    return jax.shard_map(
        body,
        mesh=mesh,
        in_specs=placed,
        out_specs=(P(("row", "col"), None), P(("row", "col"), None), P(), P(), P()),
        check_vma=False,
    )
```

```python
import jax
import jax.numpy as jnp
from jax import lax
from jax.experimental import pallas as pl
from jax.experimental.pallas import tpu as pltpu
from jax.sharding import PartitionSpec as P

MESH = pl.DeviceIdType.MESH
BF = jnp.bfloat16
F32 = jnp.float32
SLOTS = 96
ZERO = SLOTS
TN = (((0,), (0,)), ((), ()))
NT = (((1,), (1,)), ((), ()))


def mod4(v):
    return lax.rem(v, 4)


def xor4(v, d):
    v0, v1, d0, d1 = lax.rem(v, 2), lax.div(v, 2), d % 2, d // 2
    return 2 * (v1 + d1 - 2 * v1 * d1) + v0 + d0 - 2 * v0 * d0


def z_far(n):
    return mod4(2 - n + 3 * lax.div(n * (n - 1), 2))


def z_near(n):
    return mod4(n + lax.div(n * (n - 1), 2))


def dot(a, b):
    return jnp.dot(a, b, preferred_element_type=F32)


def kernel(
    rows_in, cols_in, count_in, feat_h, tiles_h, w_self_h, w_neigh_h, bias, cot_h,
    out_h, gfeat_h, gself_h, gneigh_h, gbias_h,
    A, T, X, PA, CR, Y, YR, ZS, ZR, TOT, G, ACC, BP, XR, XS, LR,
    W, M, MC, M1, MX, M2, MY, M3, ML, M4, MH, R,
    w_self, w_neigh, cot, out, gfeat, gbias, table, inv,
    lsem, osem, s1z, r1z, s1x, r1x, s3c, r3c, s3y, r3y, s3z, r3z,
    s5z, r5z, s5y, r5y, s5c, r5c, s6x, r6x, s6l, r6l, sw, rw,
):
    i = lax.axis_index("row")
    j = lax.axis_index("col")
    zl, x = lax.div(i, 4), lax.rem(i, 4)
    zh, yc = lax.div(j, 8), lax.rem(j, 8)
    y, c = lax.div(yc, 2), lax.rem(yc, 2)
    oc = 1 - c

    def dev(zl_=zl, x_=x, zh_=zh, y_=y, c_=c):
        return (zl_ * 4 + x_, zh_ * 8 + y_ * 2 + c_)

    def to_x(d):
        return dev(x_=mod4(x + d))

    def to_y(d):
        return dev(y_=mod4(y + d))

    def to_zh(d):
        return dev(zh_=mod4(zh + d))

    def to_zl(d):
        return dev(zl_=xor4(zl, d))

    def remote(src, dst, ssem, rsem, device):
        return pltpu.make_async_remote_copy(
            src_ref=src, dst_ref=dst, send_sem=ssem, recv_sem=rsem, device_id=device, device_id_type=MESH
        )

    def each3(act):
        pl.loop(1, 4)(act)

    def z1(d):
        return remote(X.at[i], X.at[i], s1z.at[d - 1], r1z.at[d - 1], to_zl(d))

    def x1(d, e):
        block = X.at[xor4(zl, d) * 4 + x]
        return remote(block, block, s1x.at[d, e - 1], r1x.at[d, e - 1], to_x(e))

    def c3(n):
        return remote(PA.at[mod4(zh + z_far(n)), oc], CR.at[n], s3c.at[n], r3c.at[n], dev(c_=oc))

    def y3(n, d):
        share = Y.at[mod4(zh + z_far(n)), mod4(y + d)]
        return remote(share, YR.at[n, d - 1], s3y.at[n, d - 1], r3y.at[n, d - 1], to_y(d))

    def z3(n):
        return remote(ZS.at[n], ZR.at[n], s3z.at[n], r3z.at[n], to_zh(z_far(n)))

    def z5(d):
        return remote(G.at[zh, c, y], G.at[zh, c, y], s5z.at[d - 1], r5z.at[d - 1], to_zh(d))

    def y5(g, d):
        block = G.at[mod4(zh + 4 - z_near(g)), c, y]
        return remote(block, block, s5y.at[g, d - 1], r5y.at[g, d - 1], to_y(d))

    def c5(g):
        slab = G.at[mod4(zh + 4 - z_near(g)), c]
        return remote(slab, slab, s5c.at[g], r5c.at[g], dev(c_=oc))

    def x6(n, d):
        share = BP.at[xor4(zl, 3 - n), mod4(x + d)]
        return remote(share, XR.at[n, d - 1], s6x.at[n, d - 1], r6x.at[n, d - 1], to_x(d))

    def l6(n):
        return remote(XS.at[n], LR.at[n], s6l.at[n], r6l.at[n], to_zl(3 - n))

    def w(k, src, dst, device):
        return remote(src, dst, sw.at[k], rw.at[k], device)

    def wc():
        return w(0, M.at[oc], MC, dev(c_=oc))

    def wx(d):
        return w(d, M1.at[mod4(x + d)], MX.at[d - 1], to_x(d))

    def wy(d):
        return w(3 + d, M2.at[mod4(y + d)], MY.at[d - 1], to_y(d))

    def wl(d):
        return w(6 + d, M3, ML.at[d - 1], to_zl(d))

    def wh(d):
        return w(9 + d, M4, MH.at[d - 1], to_zh(d))

    def vy(d):
        return w(12 + d, R.at[c, x, y], R.at[c, x, y], to_y(d))

    def vx(d):
        return w(15 + d, R.at[c, x], R.at[c, x], to_x(d))

    def vc():
        return w(19, R.at[c], R.at[c], dev(c_=oc))

    barrier = pltpu.get_barrier_semaphore()

    def greet(device):
        pl.semaphore_signal(barrier, inc=1, device_id=device, device_id_type=MESH)

    @each3
    def _(d):
        greet(to_zh(d))
        greet(to_zl(d))
        greet(to_x(d))
        greet(to_y(d))

    greet(dev(c_=oc))

    loads = [
        pltpu.make_async_copy(feat_h, X.at[i], lsem.at[0]),
        pltpu.make_async_copy(tiles_h.at[0, 0], T.at[pl.ds(0, SLOTS)], lsem.at[1]),
        pltpu.make_async_copy(w_self_h, w_self, lsem.at[2]),
        pltpu.make_async_copy(w_neigh_h, w_neigh, lsem.at[3]),
        pltpu.make_async_copy(cot_h, cot, lsem.at[4]),
    ]
    for load in loads:
        load.start()

    place_id = lax.broadcasted_iota(jnp.int32, (8, 128), 0) * 128 + lax.broadcasted_iota(jnp.int32, (8, 128), 1)
    count = count_in[0, 0]

    def note(t, found):
        r = rows_in[0, 0, t]
        place = lax.div(r, 8) * 8 + lax.rem(r, 2) * 4 + lax.div(lax.rem(r, 8), 2)
        place = jnp.where(t < count, place * 16 + cols_in[0, 0, t], -1)
        return jnp.where(place_id == place, t, found)

    table[...] = lax.fori_loop(0, SLOTS, note, jnp.full((8, 128), ZERO, jnp.int32))
    to_smem = pltpu.make_async_copy(table, inv, lsem.at[5])
    to_smem.start()
    T[ZERO] = jnp.zeros((128, 128), BF)
    ACC[...] = jnp.zeros_like(ACC)
    loads[0].wait()
    pl.semaphore_wait(barrier, 13)

    each3(lambda d: z1(d).start())
    each3(lambda d: x1(0, d).start())
    to_smem.wait()
    for load in loads[1:]:
        load.wait()

    @pl.loop(0, 4)
    def _(d):
        @pl.when(d > 0)
        def _():
            z1(d).wait_recv()
            each3(lambda e: x1(d, e).start())

        @pl.loop(d * 8, d * 8 + 8)
        def _(p):
            tile_rows = pl.ds(pl.multiple_of(p * 128, 128), 128)
            for q in range(16):
                A[tile_rows, q * 128 : (q + 1) * 128] = T[inv[lax.div(p, 8), lax.rem(p, 8) * 16 + q]]

    own_term = dot(X[i], w_self[...]) + bias[...]

    @pl.loop(0, 4)
    def _(d):
        each3(lambda e: x1(d, e).wait_recv())

    @pl.loop(0, 5)
    def _(n):
        @pl.when(n < 4)
        def _():
            zq = mod4(zh + z_far(n))
            chunk = pl.ds(pl.multiple_of(zq * 1024, 1024), 1024)
            PA[zq] = dot(A[chunk, :], X[...].reshape(2048, 256)).astype(BF).reshape(2, 4, 128, 256)
            c3(n).start()

        @pl.when(n > 0)
        def _():
            zq = mod4(zh + z_far(n - 1))
            c3(n - 1).wait_recv()
            Y[zq] = (PA[zq, c].astype(F32) + CR[n - 1].astype(F32)).astype(BF)
            each3(lambda d: y3(n - 1, d).start())

    @pl.loop(0, 4)
    def _(n):
        each3(lambda d: y3(n, d).wait_recv())
        total = Y[mod4(zh + z_far(n)), y].astype(F32)
        for d in range(3):
            total = total + YR[n, d].astype(F32)
        TOT[...] = total

        @pl.when(n < 3)
        def _():
            ZS[n] = total.astype(BF)
            z3(n).start()

    total = TOT[...]
    for n in range(3):
        z3(n).wait_recv()
        total = total + ZR[n].astype(F32)
    aggregate = total.astype(BF)

    preact = own_term + dot(aggregate, w_neigh[...])
    sigma = jax.nn.sigmoid(preact)
    grad_pre = cot[...].astype(F32) * sigma * (1.0 + preact * (1.0 - sigma))
    grad_pre_b = grad_pre.astype(BF)
    G[zh, c, y] = lax.dot_general(grad_pre_b, w_neigh[...], NT, preferred_element_type=F32).astype(BF)

    z5(1).start()
    z5(3).start()
    z5(2).start()
    each3(lambda d: y5(0, d).start())
    out[...] = (preact * sigma).astype(BF)
    save_out = pltpu.make_async_copy(out, out_h, osem.at[0])
    save_out.start()

    W[0:256] = lax.dot_general(X[i], grad_pre_b, TN, preferred_element_type=F32)
    W[256:512] = lax.dot_general(aggregate, grad_pre_b, TN, preferred_element_type=F32)
    column = jnp.sum(grad_pre, axis=0, keepdims=True)
    row_id = lax.broadcasted_iota(jnp.int32, (8, 128), 0)
    bias_tile = jnp.where(row_id == 0, column[:, :128], jnp.where(row_id == 1, column[:, 128:], 0.0))

    @pl.loop(0, 32)
    def _(q):
        part = W[pl.ds(pl.multiple_of(q * 16, 16), 16), :]
        a, b = lax.div(q, 16), lax.rem(q, 16)
        u, v = lax.div(b, 4), lax.rem(b, 4)
        M[a, u, v, 0] = part[0:8, 0:128]
        M[a, u, v, 1] = part[0:8, 128:256]
        M[a, u, v, 2] = part[8:16, 0:128]
        M[a, u, v, 3] = part[8:16, 128:256]
        M[a, u, v, 4] = bias_tile

    wc().start()
    gfeat_own = lax.dot_general(grad_pre_b, w_self[...], NT, preferred_element_type=F32)
    wc().wait_recv()
    M1[...] = M[c] + MC[...]
    each3(lambda d: wx(d).start())

    @pl.loop(0, 4)
    def _(g):
        @pl.when(g < 3)
        def _():
            z5(z_near(g + 1)).wait_recv()
            each3(lambda d: y5(g + 1, d).start())

        each3(lambda d: y5(g, d).wait_recv())
        c5(g).start()

        @pl.when(g == 0)
        def _():
            each3(lambda d: wx(d).wait_recv())
            M2[...] = M1[x] + MX[0] + MX[1] + MX[2]
            each3(lambda d: wy(d).start())

        @pl.when(g == 1)
        def _():
            each3(lambda d: wy(d).wait_recv())
            M3[...] = M2[y] + MY[0] + MY[1] + MY[2]
            each3(lambda d: wl(d).start())

        @pl.when(g == 2)
        def _():
            each3(lambda d: wl(d).wait_recv())
            M4[...] = M3[...] + ML[0] + ML[1] + ML[2]
            each3(lambda d: wh(d).start())

        c5(g).wait_recv()
        zq = mod4(zh + 4 - z_near(g))
        chunk = pl.ds(pl.multiple_of(zq * 1024, 1024), 1024)

        @pl.loop(0, 4)
        def _(n):
            part = xor4(zl, 3 - n)
            columns = pl.ds(pl.multiple_of(part * 512, 512), 512)
            ACC[part] += lax.dot_general(
                A[chunk, columns], G[zq].reshape(1024, 256), TN, preferred_element_type=F32
            )

            @pl.when(g == 3)
            def _():
                BP[part] = ACC[part].astype(BF).reshape(4, 128, 256)
                each3(lambda d: x6(n, d).start())

    each3(lambda d: wh(d).wait_recv())
    sums = M4[...] + (MH[0] + MH[1] + MH[2])
    R[c, x, y] = sums[0:4]
    each3(lambda d: vy(d).start())

    @pl.loop(0, 4)
    def _(n):
        each3(lambda d: x6(n, d).wait_recv())
        part_sum = BP[xor4(zl, 3 - n), x].astype(F32)
        for d in range(3):
            part_sum = part_sum + XR[n, d].astype(F32)
        TOT[...] = part_sum

        @pl.when(n < 3)
        def _():
            XS[n] = part_sum.astype(BF)
            l6(n).start()

        @pl.when(n == 1)
        def _():
            each3(lambda d: vy(d).wait_recv())
            each3(lambda d: vx(d).start())

    factor = 1.0 / 256.0
    gbias[...] = jnp.concatenate([sums[4, 0:1], sums[4, 1:2]], axis=1) * factor
    each3(lambda d: vx(d).wait_recv())
    vc().start()
    total = TOT[...] + gfeat_own
    for n in range(3):
        l6(n).wait_recv()
        total = total + LR[n].astype(F32)
    gfeat[...] = total.astype(BF)
    vc().wait_recv()

    @pl.loop(0, 32)
    def _(q):
        a, b = lax.div(q, 16), lax.rem(q, 16)
        u, v = lax.div(b, 4), lax.rem(b, 4)
        upper = jnp.concatenate([R[a, u, v, 0], R[a, u, v, 1]], axis=1)
        lower = jnp.concatenate([R[a, u, v, 2], R[a, u, v, 3]], axis=1)
        W[pl.ds(pl.multiple_of(q * 16, 16), 16), :] = jnp.concatenate([upper, lower], axis=0) * factor

    saves = [
        pltpu.make_async_copy(gfeat, gfeat_h, osem.at[1]),
        pltpu.make_async_copy(W.at[pl.ds(0, 256)], gself_h, osem.at[2]),
        pltpu.make_async_copy(W.at[pl.ds(256, 256)], gneigh_h, osem.at[3]),
        pltpu.make_async_copy(gbias, gbias_h, osem.at[4]),
    ]
    for save in saves:
        save.start()

    @pl.loop(0, 4)
    def _(n):
        c3(n).wait_send()
        c5(n).wait_send()

        @each3
        def _(d):
            x1(n, d).wait_send()
            y3(n, d).wait_send()
            y5(n, d).wait_send()
            x6(n, d).wait_send()

    @each3
    def _(d):
        for copy in (z1(d), z3(d - 1), z5(d), l6(d - 1), wx(d), wy(d), wl(d), wh(d), vy(d), vx(d)):
            copy.wait_send()

    wc().wait_send()
    vc().wait_send()
    save_out.wait()
    for save in saves:
        save.wait()


def hand_over(*refs):
    n = len(refs) // 2
    for k in range(n):
        refs[n + k][...] = refs[k][...]


def body(features, adj_tiles, tile_row, tile_col, tile_count, w_self, w_neigh, bias_vec, cotangent):
    smem = pl.BlockSpec(memory_space=pltpu.SMEM)
    vmem = pl.BlockSpec(memory_space=pltpu.VMEM)
    whole = pl.BlockSpec(memory_space=pl.ANY)
    dma = pltpu.SemaphoreType.DMA
    sds = jax.ShapeDtypeStruct
    results = (
        sds((128, 256), BF), sds((128, 256), BF), sds((256, 256), F32), sds((256, 256), F32), sds((1, 256), F32),
    )
    held = pl.pallas_call(
        kernel,
        out_shape=results,
        in_specs=[smem, smem, smem, whole, whole, whole, whole, vmem, whole],
        out_specs=(whole,) * 5,
        scratch_shapes=[
            pltpu.VMEM((4096, 2048), BF),
            pltpu.VMEM((SLOTS + 1, 128, 128), BF),
            pltpu.VMEM((16, 128, 256), BF),
            pltpu.VMEM((4, 2, 4, 128, 256), BF),
            pltpu.VMEM((4, 4, 128, 256), BF),
            pltpu.VMEM((4, 4, 128, 256), BF),
            pltpu.VMEM((4, 3, 128, 256), BF),
            pltpu.VMEM((3, 128, 256), BF),
            pltpu.VMEM((3, 128, 256), BF),
            pltpu.VMEM((128, 256), F32),
            pltpu.VMEM((4, 2, 4, 128, 256), BF),
            pltpu.VMEM((4, 512, 256), F32),
            pltpu.VMEM((4, 4, 128, 256), BF),
            pltpu.VMEM((4, 3, 128, 256), BF),
            pltpu.VMEM((3, 128, 256), BF),
            pltpu.VMEM((3, 128, 256), BF),
            pltpu.VMEM((512, 256), F32),
            pltpu.VMEM((2, 4, 4, 5, 8, 128), F32),
            pltpu.VMEM((4, 4, 5, 8, 128), F32),
            pltpu.VMEM((4, 4, 5, 8, 128), F32),
            pltpu.VMEM((3, 4, 5, 8, 128), F32),
            pltpu.VMEM((4, 5, 8, 128), F32),
            pltpu.VMEM((3, 5, 8, 128), F32),
            pltpu.VMEM((5, 8, 128), F32),
            pltpu.VMEM((3, 5, 8, 128), F32),
            pltpu.VMEM((5, 8, 128), F32),
            pltpu.VMEM((3, 5, 8, 128), F32),
            pltpu.VMEM((2, 4, 4, 4, 8, 128), F32),
            pltpu.VMEM((256, 256), BF),
            pltpu.VMEM((256, 256), BF),
            pltpu.VMEM((128, 256), BF),
            pltpu.VMEM((128, 256), BF),
            pltpu.VMEM((128, 256), BF),
            pltpu.VMEM((1, 256), F32),
            pltpu.VMEM((8, 128), jnp.int32),
            pltpu.SMEM((8, 128), jnp.int32),
            dma((6,)), dma((5,)),
            dma((3,)), dma((3,)), dma((4, 3)), dma((4, 3)),
            dma((4,)), dma((4,)), dma((4, 3)), dma((4, 3)), dma((3,)), dma((3,)),
            dma((3,)), dma((3,)), dma((4, 3)), dma((4, 3)), dma((4,)), dma((4,)),
            dma((4, 3)), dma((4, 3)), dma((3,)), dma((3,)),
            dma((20,)), dma((20,)),
        ],
        compiler_params=pltpu.CompilerParams(
            collective_id=0, has_side_effects=True, vmem_limit_bytes=60 * 2**20
        ),
    )(
        tile_row, tile_col, tile_count, features, adj_tiles, w_self, w_neigh, bias_vec.reshape(1, 256), cotangent
    )
    out, gfeat, gself, gneigh, gbias = pl.pallas_call(
        hand_over,
        out_shape=results,
        in_specs=[vmem] * 5,
        out_specs=(vmem,) * 5,
    )(*held)
    return out, gfeat, gself, gneigh, gbias.reshape(256)


def solution(mesh):
    placed = (
        P(("row", "col"), None),
        P("row", "col", None, None, None),
        P("row", "col", None),
        P("row", "col", None),
        P("row", "col"),
        P(),
        P(),
        P(),
        P(("row", "col"), None),
    )
    return jax.shard_map(
        body,
        mesh=mesh,
        in_specs=placed,
        out_specs=(P(("row", "col"), None), P(("row", "col"), None), P(), P(), P()),
        check_vma=False,
    )
```

```python
import jax
import jax.numpy as jnp
from jax import lax
from jax.experimental import pallas as pl
from jax.experimental.pallas import tpu as pltpu
from jax.sharding import PartitionSpec as P

MESH = pl.DeviceIdType.MESH
BF = jnp.bfloat16
F32 = jnp.float32
SLOTS = 96
ZERO = SLOTS
TN = (((0,), (0,)), ((), ()))
NT = (((1,), (1,)), ((), ()))


def mod4(v):
    return lax.rem(v, 4)


def xor4(v, d):
    v0, v1, d0, d1 = lax.rem(v, 2), lax.div(v, 2), d % 2, d // 2
    return 2 * (v1 + d1 - 2 * v1 * d1) + v0 + d0 - 2 * v0 * d0


def z_far(n):
    return mod4(2 - n + 3 * lax.div(n * (n - 1), 2))


def z_near(n):
    return mod4(n + lax.div(n * (n - 1), 2))


def dot(a, b):
    return jnp.dot(a, b, preferred_element_type=F32)


def kernel(
    rows_h, cols_h, count_h, feat_h, tiles_h, w_self_h, w_neigh_h, bias_h, cot_h,
    out_h, gfeat_h, gself_h, gneigh_h, gbias_h,
    A, T, X, PA, CR, Y, YR, ZS, ZR, TOT, G, ACC, BP, XR, XS, LR,
    W, M, MC, M1, MX, M2, MY, M3, ML, M4, MH, R,
    w_self, w_neigh, bias, cot, out, gfeat, gbias, rows_in, cols_in, count_in, table, inv,
    lsem, osem, s1z, r1z, s1x, r1x, s3c, r3c, s3y, r3y, s3z, r3z,
    s5z, r5z, s5y, r5y, s5c, r5c, s6x, r6x, s6l, r6l, sw, rw,
):
    i = lax.axis_index("row")
    j = lax.axis_index("col")
    zl, x = lax.div(i, 4), lax.rem(i, 4)
    zh, yc = lax.div(j, 8), lax.rem(j, 8)
    y, c = lax.div(yc, 2), lax.rem(yc, 2)
    oc = 1 - c

    def dev(zl_=zl, x_=x, zh_=zh, y_=y, c_=c):
        return (zl_ * 4 + x_, zh_ * 8 + y_ * 2 + c_)

    def to_x(d):
        return dev(x_=mod4(x + d))

    def to_y(d):
        return dev(y_=mod4(y + d))

    def to_zh(d):
        return dev(zh_=mod4(zh + d))

    def to_zl(d):
        return dev(zl_=xor4(zl, d))

    def remote(src, dst, ssem, rsem, device):
        return pltpu.make_async_remote_copy(
            src_ref=src, dst_ref=dst, send_sem=ssem, recv_sem=rsem, device_id=device, device_id_type=MESH
        )

    def each3(act):
        pl.loop(1, 4)(act)

    def z1(d):
        return remote(X.at[i], X.at[i], s1z.at[d - 1], r1z.at[d - 1], to_zl(d))

    def x1(d, e):
        block = X.at[xor4(zl, d) * 4 + x]
        return remote(block, block, s1x.at[d, e - 1], r1x.at[d, e - 1], to_x(e))

    def c3(n):
        return remote(PA.at[mod4(zh + z_far(n)), oc], CR.at[n], s3c.at[n], r3c.at[n], dev(c_=oc))

    def y3(n, d):
        share = Y.at[mod4(zh + z_far(n)), mod4(y + d)]
        return remote(share, YR.at[n, d - 1], s3y.at[n, d - 1], r3y.at[n, d - 1], to_y(d))

    def half(ref, k):
        return ref.at[pl.ds(64 * k, 64)]

    def z3(n):
        src = half(ZS.at[0], n) if n < 2 else ZS.at[n - 1]
        dst = half(ZR.at[0], n) if n < 2 else ZR.at[n - 1]
        return remote(src, dst, s3z.at[n], r3z.at[n], to_zh(1 + 2 * (n % 2)))

    def z5(k):
        if k < 2:
            block = G.at[zh, c, y]
        else:
            block = half(G.at[mod4(zh + 3 - 2 * (k % 2)), c, y], k % 2)
        return remote(block, block, s5z.at[k], r5z.at[k], to_zh(1 + 2 * (k % 2)))

    def y5(g, d):
        block = G.at[mod4(zh + 4 - z_near(g)), c, y]
        return remote(block, block, s5y.at[g, d - 1], r5y.at[g, d - 1], to_y(d))

    def c5(g):
        slab = G.at[mod4(zh + 4 - z_near(g)), c]
        return remote(slab, slab, s5c.at[g], r5c.at[g], dev(c_=oc))

    def x6(n, d):
        share = BP.at[xor4(zl, 3 - n), mod4(x + d)]
        return remote(share, XR.at[n, d - 1], s6x.at[n, d - 1], r6x.at[n, d - 1], to_x(d))

    def l6(n):
        return remote(XS.at[n], LR.at[n], s6l.at[n], r6l.at[n], to_zl(3 - n))

    def w(k, src, dst, device):
        return remote(src, dst, sw.at[k], rw.at[k], device)

    def wc():
        return w(0, M.at[oc], MC, dev(c_=oc))

    def wx(d):
        return w(d, M1.at[mod4(x + d)], MX.at[d - 1], to_x(d))

    def wy(d):
        return w(3 + d, M2.at[mod4(y + d)], MY.at[d - 1], to_y(d))

    def wl(d):
        return w(6 + d, M3, ML.at[d - 1], to_zl(d))

    def wh(k):
        return w(20 if k == 2 else 10 + k, MH.at[0] if k == 2 else M4, MH.at[k], to_zh(1 + 2 * (k % 2)))

    def vx(d):
        return w(12 + d, R.at[c, y, x], R.at[c, y, x], to_x(d))

    def vy(d):
        return w(15 + d, R.at[c, y], R.at[c, y], to_y(d))

    def vc():
        return w(19, R.at[c], R.at[c], dev(c_=oc))

    barrier = pltpu.get_barrier_semaphore()

    def greet(device):
        pl.semaphore_signal(barrier, inc=1, device_id=device, device_id_type=MESH)

    @each3
    def _(d):
        greet(to_zl(d))
        greet(to_x(d))
        greet(to_y(d))

    greet(dev(c_=oc))
    greet(to_zh(1))
    greet(to_zh(3))

    loads = [
        pltpu.make_async_copy(feat_h, X.at[i], lsem.at[0]),
        pltpu.make_async_copy(tiles_h.at[0, 0], T.at[pl.ds(0, SLOTS)], lsem.at[1]),
        pltpu.make_async_copy(w_self_h, w_self, lsem.at[2]),
        pltpu.make_async_copy(w_neigh_h, w_neigh, lsem.at[3]),
        pltpu.make_async_copy(cot_h, cot, lsem.at[4]),
        pltpu.make_async_copy(bias_h, bias, lsem.at[5]),
        pltpu.make_async_copy(rows_h, rows_in, lsem.at[6]),
        pltpu.make_async_copy(cols_h, cols_in, lsem.at[7]),
        pltpu.make_async_copy(count_h, count_in, lsem.at[8]),
    ]
    for load in loads:
        load.start()

    for load in loads[6:]:
        load.wait()
    place_id = lax.broadcasted_iota(jnp.int32, (8, 128), 0) * 128 + lax.broadcasted_iota(jnp.int32, (8, 128), 1)
    count = count_in[0, 0]

    def note(t, found):
        r = rows_in[0, 0, t]
        place = lax.div(r, 8) * 8 + lax.rem(r, 2) * 4 + lax.div(lax.rem(r, 8), 2)
        place = jnp.where(t < count, place * 16 + cols_in[0, 0, t], -1)
        return jnp.where(place_id == place, t, found)

    table[...] = lax.fori_loop(0, SLOTS, note, jnp.full((8, 128), ZERO, jnp.int32))
    to_smem = pltpu.make_async_copy(table, inv, lsem.at[9])
    to_smem.start()
    T[ZERO] = jnp.zeros((128, 128), BF)
    ACC[...] = jnp.zeros_like(ACC)
    loads[0].wait()
    pl.semaphore_wait(barrier, 12)

    each3(lambda d: z1(d).start())
    each3(lambda d: x1(0, d).start())
    to_smem.wait()
    for load in loads[1:6]:
        load.wait()

    @pl.loop(0, 4)
    def _(d):
        @pl.when(d > 0)
        def _():
            z1(d).wait_recv()
            each3(lambda e: x1(d, e).start())

        @pl.loop(d * 8, d * 8 + 8)
        def _(p):
            tile_rows = pl.ds(pl.multiple_of(p * 128, 128), 128)
            for q in range(16):
                A[tile_rows, q * 128 : (q + 1) * 128] = T[inv[lax.div(p, 8), lax.rem(p, 8) * 16 + q]]

    own_term = dot(X[i], w_self[...]) + bias[...]

    @pl.loop(0, 4)
    def _(d):
        each3(lambda e: x1(d, e).wait_recv())

    @pl.loop(0, 5)
    def _(n):
        @pl.when(n < 4)
        def _():
            zq = mod4(zh + z_far(n))
            chunk = pl.ds(pl.multiple_of(zq * 1024, 1024), 1024)
            PA[zq] = dot(A[chunk, :], X[...].reshape(2048, 256)).astype(BF).reshape(2, 4, 128, 256)
            c3(n).start()

        @pl.when(n > 0)
        def _():
            zq = mod4(zh + z_far(n - 1))
            c3(n - 1).wait_recv()
            Y[zq] = (PA[zq, c].astype(F32) + CR[n - 1].astype(F32)).astype(BF)
            each3(lambda d: y3(n - 1, d).start())

    @pl.loop(0, 4)
    def _(n):
        each3(lambda d: y3(n, d).wait_recv())
        total = Y[mod4(zh + z_far(n)), y].astype(F32)
        for d in range(3):
            total = total + YR[n, d].astype(F32)
        TOT[...] = total

        @pl.when(n == 0)
        def _():
            ZS[0] = total.astype(BF)
            z3(0).start()
            z3(1).start()

        for k in range(2):

            @pl.when(n == 1 + k)
            def _():
                z3(k).wait_recv()
                near = slice(64 * k, 64 * k + 64)
                TOT[near] += ZR[0, near].astype(F32)
                ZS[1 + k] = TOT[...].astype(BF)
                z3(2 + k).start()

    z3(2).wait_recv()
    z3(3).wait_recv()
    total = TOT[...] + ZR[1].astype(F32) + ZR[2].astype(F32)
    aggregate = total.astype(BF)

    preact = own_term + dot(aggregate, w_neigh[...])
    sigma = jax.nn.sigmoid(preact)
    grad_pre = cot[...].astype(F32) * sigma * (1.0 + preact * (1.0 - sigma))
    grad_pre_b = grad_pre.astype(BF)
    G[zh, c, y] = lax.dot_general(grad_pre_b, w_neigh[...], NT, preferred_element_type=F32).astype(BF)

    z5(0).start()
    z5(1).start()
    each3(lambda d: y5(0, d).start())
    out[...] = (preact * sigma).astype(BF)
    save_out = pltpu.make_async_copy(out, out_h, osem.at[0])
    save_out.start()

    W[0:256] = lax.dot_general(X[i], grad_pre_b, TN, preferred_element_type=F32)
    W[256:512] = lax.dot_general(aggregate, grad_pre_b, TN, preferred_element_type=F32)
    column = jnp.sum(grad_pre, axis=0, keepdims=True)
    row_id = lax.broadcasted_iota(jnp.int32, (8, 128), 0)
    bias_tile = jnp.where(row_id == 0, column[:, :128], jnp.where(row_id == 1, column[:, 128:], 0.0))

    @pl.loop(0, 32)
    def _(q):
        part = W[pl.ds(pl.multiple_of(q * 16, 16), 16), :]
        a, b = lax.div(q, 16), lax.rem(q, 16)
        u, v = lax.div(b, 4), lax.rem(b, 4)
        M[a, u, v, 0] = part[0:8, 0:128]
        M[a, u, v, 1] = part[0:8, 128:256]
        M[a, u, v, 2] = part[8:16, 0:128]
        M[a, u, v, 3] = part[8:16, 128:256]
        M[a, u, v, 4] = bias_tile

    wc().start()
    gfeat_own = lax.dot_general(grad_pre_b, w_self[...], NT, preferred_element_type=F32)
    wc().wait_recv()
    M1[...] = M[c] + MC[...]
    each3(lambda d: wx(d).start())

    each3(lambda d: wx(d).wait_recv())
    M2[...] = M1[x] + MX[0] + MX[1] + MX[2]
    each3(lambda d: wy(d).start())

    @pl.loop(0, 4)
    def _(g):
        for k in range(2):

            @pl.when(g == k)
            def _():
                z5(k).wait_recv()
                z5(2 + k).start()

        @pl.when(g == 2)
        def _():
            z5(2).wait_recv()
            z5(3).wait_recv()

        @pl.when(g < 3)
        def _():
            each3(lambda d: y5(g + 1, d).start())

        @pl.when(g == 1)
        def _():
            each3(lambda d: wy(d).wait_recv())
            M3[...] = M2[y] + MY[0] + MY[1] + MY[2]
            each3(lambda d: wl(d).start())

        @pl.when(g == 2)
        def _():
            each3(lambda d: wl(d).wait_recv())
            M4[...] = (M3[...] + ML[0]) + (ML[1] + ML[2])
            wh(0).start()
            wh(1).start()

        @pl.when(g == 3)
        def _():
            wh(0).wait_recv()
            wh(2).start()

        each3(lambda d: y5(g, d).wait_recv())
        c5(g).start()
        c5(g).wait_recv()
        zq = mod4(zh + 4 - z_near(g))
        chunk = pl.ds(pl.multiple_of(zq * 1024, 1024), 1024)

        @pl.loop(0, 4)
        def _(n):
            part = xor4(zl, 3 - n)
            columns = pl.ds(pl.multiple_of(part * 512, 512), 512)
            ACC[part] += lax.dot_general(
                A[chunk, columns], G[zq].reshape(1024, 256), TN, preferred_element_type=F32
            )

            @pl.when(g == 3)
            def _():
                BP[part] = ACC[part].astype(BF).reshape(4, 128, 256)

            @pl.when((g == 3) & (n < 2))
            def _():
                each3(lambda d: x6(n, d).start())

    wh(1).wait_recv()
    wh(2).wait_recv()
    sums = (M4[...] + MH[2]) + (MH[0] + MH[1])
    R[c, y, x] = sums[0:4]
    each3(lambda d: vx(d).start())
    each3(lambda d: x6(2, d).start())
    each3(lambda d: x6(3, d).start())

    @pl.loop(0, 4)
    def _(n):
        each3(lambda d: x6(n, d).wait_recv())
        part_sum = BP[xor4(zl, 3 - n), x].astype(F32)
        for d in range(3):
            part_sum = part_sum + XR[n, d].astype(F32)
        TOT[...] = part_sum

        @pl.when(n < 3)
        def _():
            XS[n] = part_sum.astype(BF)
            l6(n).start()

        @pl.when(n == 1)
        def _():
            each3(lambda d: vx(d).wait_recv())
            each3(lambda d: vy(d).start())

    factor = 1.0 / 256.0
    gbias[...] = jnp.concatenate([sums[4, 0:1], sums[4, 1:2]], axis=1) * factor
    each3(lambda d: vy(d).wait_recv())
    vc().start()

    def assemble(a):
        @pl.loop(0, 16)
        def _(q):
            u, v = lax.div(q, 4), lax.rem(q, 4)
            upper = jnp.concatenate([R[a, v, u, 0], R[a, v, u, 1]], axis=1)
            lower = jnp.concatenate([R[a, v, u, 2], R[a, v, u, 3]], axis=1)
            rows = pl.ds(pl.multiple_of(a * 256 + q * 16, 16), 16)
            W[rows, :] = jnp.concatenate([upper, lower], axis=0) * factor

    assemble(c)
    total = TOT[...] + gfeat_own
    for n in range(3):
        l6(n).wait_recv()
        total = total + LR[n].astype(F32)
    gfeat[...] = total.astype(BF)
    vc().wait_recv()
    assemble(oc)
    saves = [
        pltpu.make_async_copy(gfeat, gfeat_h, osem.at[1]),
        pltpu.make_async_copy(W.at[pl.ds(0, 256)], gself_h, osem.at[2]),
        pltpu.make_async_copy(W.at[pl.ds(256, 256)], gneigh_h, osem.at[3]),
        pltpu.make_async_copy(gbias, gbias_h, osem.at[4]),
    ]
    for save in saves:
        save.start()

    @pl.loop(0, 4)
    def _(n):
        c3(n).wait_send()
        c5(n).wait_send()

        @each3
        def _(d):
            x1(n, d).wait_send()
            y3(n, d).wait_send()
            y5(n, d).wait_send()
            x6(n, d).wait_send()

    @each3
    def _(d):
        for copy in (z1(d), l6(d - 1), wx(d), wy(d), wl(d), vy(d), vx(d)):
            copy.wait_send()

    for copy in (wc(), vc(), wh(0), wh(1), wh(2), *map(z3, range(4)), *map(z5, range(4))):
        copy.wait_send()
    save_out.wait()
    for save in saves:
        save.wait()


def hand_over(*refs):
    n = len(refs) // 2
    for k in range(n):
        refs[n + k][...] = refs[k][...]


def body(features, adj_tiles, tile_row, tile_col, tile_count, w_self, w_neigh, bias_vec, cotangent):
    vmem = pl.BlockSpec(memory_space=pltpu.VMEM)
    whole = pl.BlockSpec(memory_space=pl.ANY)
    dma = pltpu.SemaphoreType.DMA
    sds = jax.ShapeDtypeStruct
    results = (
        sds((128, 256), BF), sds((128, 256), BF), sds((256, 256), F32), sds((256, 256), F32), sds((1, 256), F32),
    )
    held = pl.pallas_call(
        kernel,
        out_shape=results,
        in_specs=[whole] * 9,
        out_specs=(whole,) * 5,
        scratch_shapes=[
            pltpu.VMEM((4096, 2048), BF),
            pltpu.VMEM((SLOTS + 1, 128, 128), BF),
            pltpu.VMEM((16, 128, 256), BF),
            pltpu.VMEM((4, 2, 4, 128, 256), BF),
            pltpu.VMEM((4, 4, 128, 256), BF),
            pltpu.VMEM((4, 4, 128, 256), BF),
            pltpu.VMEM((4, 3, 128, 256), BF),
            pltpu.VMEM((3, 128, 256), BF),
            pltpu.VMEM((3, 128, 256), BF),
            pltpu.VMEM((128, 256), F32),
            pltpu.VMEM((4, 2, 4, 128, 256), BF),
            pltpu.VMEM((4, 512, 256), F32),
            pltpu.VMEM((4, 4, 128, 256), BF),
            pltpu.VMEM((4, 3, 128, 256), BF),
            pltpu.VMEM((3, 128, 256), BF),
            pltpu.VMEM((3, 128, 256), BF),
            pltpu.VMEM((512, 256), F32),
            pltpu.VMEM((2, 4, 4, 5, 8, 128), F32),
            pltpu.VMEM((4, 4, 5, 8, 128), F32),
            pltpu.VMEM((4, 4, 5, 8, 128), F32),
            pltpu.VMEM((3, 4, 5, 8, 128), F32),
            pltpu.VMEM((4, 5, 8, 128), F32),
            pltpu.VMEM((3, 5, 8, 128), F32),
            pltpu.VMEM((5, 8, 128), F32),
            pltpu.VMEM((3, 5, 8, 128), F32),
            pltpu.VMEM((5, 8, 128), F32),
            pltpu.VMEM((3, 5, 8, 128), F32),
            pltpu.VMEM((2, 4, 4, 4, 8, 128), F32),
            pltpu.VMEM((256, 256), BF),
            pltpu.VMEM((256, 256), BF),
            pltpu.VMEM((1, 256), F32),
            pltpu.VMEM((128, 256), BF),
            pltpu.VMEM((128, 256), BF),
            pltpu.VMEM((128, 256), BF),
            pltpu.VMEM((1, 256), F32),
            pltpu.SMEM((1, 1, SLOTS), jnp.int32),
            pltpu.SMEM((1, 1, SLOTS), jnp.int32),
            pltpu.SMEM((1, 1), jnp.int32),
            pltpu.VMEM((8, 128), jnp.int32),
            pltpu.SMEM((8, 128), jnp.int32),
            dma((10,)), dma((5,)),
            dma((3,)), dma((3,)), dma((4, 3)), dma((4, 3)),
            dma((4,)), dma((4,)), dma((4, 3)), dma((4, 3)), dma((4,)), dma((4,)),
            dma((4,)), dma((4,)), dma((4, 3)), dma((4, 3)), dma((4,)), dma((4,)),
            dma((4, 3)), dma((4, 3)), dma((3,)), dma((3,)),
            dma((21,)), dma((21,)),
        ],
        compiler_params=pltpu.CompilerParams(
            collective_id=0, has_side_effects=True, vmem_limit_bytes=60 * 2**20
        ),
    )(
        tile_row, tile_col, tile_count, features, adj_tiles, w_self, w_neigh, bias_vec.reshape(1, 256), cotangent
    )
    out, gfeat, gself, gneigh, gbias = pl.pallas_call(
        hand_over,
        out_shape=results,
        in_specs=[vmem] * 5,
        out_specs=(vmem,) * 5,
    )(*held)
    return out, gfeat, gself, gneigh, gbias.reshape(256)


def solution(mesh):
    placed = (
        P(("row", "col"), None),
        P("row", "col", None, None, None),
        P("row", "col", None),
        P("row", "col", None),
        P("row", "col"),
        P(),
        P(),
        P(),
        P(("row", "col"), None),
    )
    return jax.shard_map(
        body,
        mesh=mesh,
        in_specs=placed,
        out_specs=(P(("row", "col"), None), P(("row", "col"), None), P(), P(), P()),
        check_vma=False,
    )
```

```python
import jax
import jax.numpy as jnp
from jax import lax
from jax.experimental import pallas as pl
from jax.experimental.pallas import tpu as pltpu
from jax.sharding import PartitionSpec as P

MESH = pl.DeviceIdType.MESH
BF = jnp.bfloat16
F32 = jnp.float32
SLOTS = 96
ZERO = SLOTS
TN = (((0,), (0,)), ((), ()))
NT = (((1,), (1,)), ((), ()))


def mod4(v):
    return lax.rem(v, 4)


def xor4(v, d):
    v0, v1, d0, d1 = lax.rem(v, 2), lax.div(v, 2), d % 2, d // 2
    return 2 * (v1 + d1 - 2 * v1 * d1) + v0 + d0 - 2 * v0 * d0


def z_far(n):
    return mod4(2 - n + 3 * lax.div(n * (n - 1), 2))


def z_near(n):
    return mod4(n + lax.div(n * (n - 1), 2))


def dot(a, b):
    return jnp.dot(a, b, preferred_element_type=F32)


def kernel(
    rows_h, cols_h, count_h, feat_h, tiles_h, w_self_h, w_neigh_h, bias_h, cot_h,
    out_h, gfeat_h, gself_h, gneigh_h, gbias_h,
    A, T, X, PA, CR, Y, YR, ZS, ZR, TOT, G, ACC, BP, XR, XS, LR,
    W, M, MC, M1, MX, M2, MY, M3, ML, M4, MH, R,
    w_self, w_neigh, bias, cot, out, gfeat, gbias, rows_in, cols_in, count_in, table, inv,
    lsem, osem, s1z, r1z, s1x, r1x, s3c, r3c, s3y, r3y, s3z, r3z,
    s5z, r5z, s5y, r5y, s5c, r5c, s6x, r6x, s6l, r6l, sw, rw,
):
    i = lax.axis_index("row")
    j = lax.axis_index("col")
    zl, x = lax.div(i, 4), lax.rem(i, 4)
    zh, yc = lax.div(j, 8), lax.rem(j, 8)
    y, c = lax.div(yc, 2), lax.rem(yc, 2)
    oc = 1 - c

    def dev(zl_=zl, x_=x, zh_=zh, y_=y, c_=c):
        return (zl_ * 4 + x_, zh_ * 8 + y_ * 2 + c_)

    def to_x(d):
        return dev(x_=mod4(x + d))

    def to_y(d):
        return dev(y_=mod4(y + d))

    def to_zh(d):
        return dev(zh_=mod4(zh + d))

    def to_zl(d):
        return dev(zl_=xor4(zl, d))

    def remote(src, dst, ssem, rsem, device):
        return pltpu.make_async_remote_copy(
            src_ref=src, dst_ref=dst, send_sem=ssem, recv_sem=rsem, device_id=device, device_id_type=MESH
        )

    def each3(act):
        pl.loop(1, 4)(lambda k: act(1 + lax.rem(k, 3)))

    def z1(d):
        return remote(X.at[i], X.at[i], s1z.at[d - 1], r1z.at[d - 1], to_zl(d))

    def x1(d, e):
        block = X.at[xor4(zl, d) * 4 + x]
        return remote(block, block, s1x.at[d, e - 1], r1x.at[d, e - 1], to_x(e))

    def c3(n):
        return remote(PA.at[mod4(zh + z_far(n)), oc], CR.at[n], s3c.at[n], r3c.at[n], dev(c_=oc))

    def y3(n, d):
        share = Y.at[mod4(zh + z_far(n)), mod4(y + d)]
        return remote(share, YR.at[n, d - 1], s3y.at[n, d - 1], r3y.at[n, d - 1], to_y(d))

    def half(ref, k):
        return ref.at[pl.ds(64 * k, 64)]

    def z3(n):
        src = half(ZS.at[0], n) if n < 2 else ZS.at[n - 1]
        dst = half(ZR.at[0], n) if n < 2 else ZR.at[n - 1]
        return remote(src, dst, s3z.at[n], r3z.at[n], to_zh(1 + 2 * (n % 2)))

    def z5(k):
        if k < 2:
            block = G.at[zh, c, y]
        else:
            block = half(G.at[mod4(zh + 3 - 2 * (k % 2)), c, y], k % 2)
        return remote(block, block, s5z.at[k], r5z.at[k], to_zh(1 + 2 * (k % 2)))

    def y5(g, d):
        block = G.at[mod4(zh + 4 - z_near(g)), c, y]
        return remote(block, block, s5y.at[g, d - 1], r5y.at[g, d - 1], to_y(d))

    def c5(g):
        slab = G.at[mod4(zh + 4 - z_near(g)), c]
        return remote(slab, slab, s5c.at[g], r5c.at[g], dev(c_=oc))

    def x6(n, d):
        share = BP.at[xor4(zl, 3 - n), mod4(x + d)]
        return remote(share, XR.at[n, d - 1], s6x.at[n, d - 1], r6x.at[n, d - 1], to_x(d))

    def l6(n):
        return remote(XS.at[n], LR.at[n], s6l.at[n], r6l.at[n], to_zl(3 - n))

    def w(k, src, dst, device):
        return remote(src, dst, sw.at[k], rw.at[k], device)

    def wc():
        return w(0, M.at[oc], MC, dev(c_=oc))

    def wx(d):
        return w(d, M1.at[mod4(x + d)], MX.at[d - 1], to_x(d))

    def wy(d):
        return w(3 + d, M2.at[mod4(y + d)], MY.at[d - 1], to_y(d))

    def wl(d):
        return w(6 + d, M3, ML.at[d - 1], to_zl(d))

    def wh(k):
        return w(20 if k == 2 else 10 + k, MH.at[0] if k == 2 else M4, MH.at[k], to_zh(1 + 2 * (k % 2)))

    def vx(d):
        return w(12 + d, R.at[c, y, x], R.at[c, y, x], to_x(d))

    def vy(d):
        return w(15 + d, R.at[c, y], R.at[c, y], to_y(d))

    def vc():
        return w(19, R.at[c], R.at[c], dev(c_=oc))

    barrier = pltpu.get_barrier_semaphore()

    def greet(device):
        pl.semaphore_signal(barrier, inc=1, device_id=device, device_id_type=MESH)

    @each3
    def _(d):
        greet(to_zl(d))
        greet(to_x(d))
        greet(to_y(d))

    greet(dev(c_=oc))
    greet(to_zh(1))
    greet(to_zh(3))

    loads = [
        pltpu.make_async_copy(feat_h, X.at[i], lsem.at[0]),
        pltpu.make_async_copy(tiles_h.at[0, 0], T.at[pl.ds(0, SLOTS)], lsem.at[1]),
        pltpu.make_async_copy(w_self_h, w_self, lsem.at[2]),
        pltpu.make_async_copy(w_neigh_h, w_neigh, lsem.at[3]),
        pltpu.make_async_copy(cot_h, cot, lsem.at[4]),
        pltpu.make_async_copy(bias_h, bias, lsem.at[5]),
        pltpu.make_async_copy(rows_h, rows_in, lsem.at[6]),
        pltpu.make_async_copy(cols_h, cols_in, lsem.at[7]),
        pltpu.make_async_copy(count_h, count_in, lsem.at[8]),
    ]
    for load in loads:
        load.start()

    for load in loads[6:]:
        load.wait()
    place_id = lax.broadcasted_iota(jnp.int32, (8, 128), 0) * 128 + lax.broadcasted_iota(jnp.int32, (8, 128), 1)
    count = count_in[0, 0]

    def note(t, found):
        r = rows_in[0, 0, t]
        place = lax.div(r, 8) * 8 + lax.rem(r, 2) * 4 + lax.div(lax.rem(r, 8), 2)
        place = jnp.where(t < count, place * 16 + cols_in[0, 0, t], -1)
        return jnp.where(place_id == place, t, found)

    table[...] = lax.fori_loop(0, SLOTS, note, jnp.full((8, 128), ZERO, jnp.int32))
    to_smem = pltpu.make_async_copy(table, inv, lsem.at[9])
    to_smem.start()
    T[ZERO] = jnp.zeros((128, 128), BF)
    ACC[...] = jnp.zeros_like(ACC)
    loads[0].wait()
    pl.semaphore_wait(barrier, 12)

    pl.loop(0, 3)(lambda k: z1(3 - k).start())
    each3(lambda d: x1(0, d).start())
    to_smem.wait()
    for load in loads[1:6]:
        load.wait()

    @pl.loop(0, 4)
    def _(n):
        @pl.when(n > 0)
        def _():
            z1(4 - n).wait_recv()
            each3(lambda e: x1(4 - n, e).start())

        @pl.loop(n * 8, n * 8 + 8)
        def _(p):
            tile_rows = pl.ds(pl.multiple_of(p * 128, 128), 128)
            for q in range(16):
                A[tile_rows, q * 128 : (q + 1) * 128] = T[inv[lax.div(p, 8), lax.rem(p, 8) * 16 + q]]

    own_term = dot(X[i], w_self[...]) + bias[...]

    @pl.loop(0, 4)
    def _(d):
        each3(lambda e: x1(d, e).wait_recv())

    @pl.loop(0, 5)
    def _(n):
        @pl.when(n < 4)
        def _():
            zq = mod4(zh + z_far(n))
            chunk = pl.ds(pl.multiple_of(zq * 1024, 1024), 1024)
            PA[zq] = dot(A[chunk, :], X[...].reshape(2048, 256)).astype(BF).reshape(2, 4, 128, 256)
            c3(n).start()

        @pl.when(n > 0)
        def _():
            zq = mod4(zh + z_far(n - 1))
            c3(n - 1).wait_recv()
            Y[zq] = (PA[zq, c].astype(F32) + CR[n - 1].astype(F32)).astype(BF)
            each3(lambda d: y3(n - 1, d).start())

    @pl.loop(0, 4)
    def _(n):
        each3(lambda d: y3(n, d).wait_recv())
        total = Y[mod4(zh + z_far(n)), y].astype(F32)
        for d in range(3):
            total = total + YR[n, d].astype(F32)
        TOT[...] = total

        @pl.when(n == 0)
        def _():
            ZS[0] = total.astype(BF)
            z3(0).start()
            z3(1).start()

        for k in range(2):

            @pl.when(n == 1 + k)
            def _():
                z3(k).wait_recv()
                near = slice(64 * k, 64 * k + 64)
                TOT[near] += ZR[0, near].astype(F32)
                ZS[1 + k] = TOT[...].astype(BF)
                z3(2 + k).start()

    z3(2).wait_recv()
    z3(3).wait_recv()
    total = TOT[...] + ZR[1].astype(F32) + ZR[2].astype(F32)
    aggregate = total.astype(BF)

    preact = own_term + dot(aggregate, w_neigh[...])
    sigma = jax.nn.sigmoid(preact)
    grad_pre = cot[...].astype(F32) * sigma * (1.0 + preact * (1.0 - sigma))
    grad_pre_b = grad_pre.astype(BF)
    G[zh, c, y] = lax.dot_general(grad_pre_b, w_neigh[...], NT, preferred_element_type=F32).astype(BF)

    z5(0).start()
    z5(1).start()
    each3(lambda d: y5(0, d).start())
    out[...] = (preact * sigma).astype(BF)
    save_out = pltpu.make_async_copy(out, out_h, osem.at[0])
    save_out.start()

    def split(value):
        high = value.astype(BF).astype(F32)
        return jnp.concatenate([high, value - high], axis=0).astype(BF)

    def joined(tile):
        return tile[0:8] + tile[8:16]

    def keep(ref, total):
        ref[...] = total.astype(BF)
        lead = total.ndim - 3
        tile = split(joined(total[(0,) * lead + (2,)]))
        ref[(slice(None),) * lead + (2,)] = jnp.broadcast_to(tile, total.shape[:lead] + tile.shape)

    def wide(value):
        return value.astype(F32)

    W[0:256] = lax.dot_general(X[i], grad_pre_b, TN, preferred_element_type=F32)
    W[256:512] = lax.dot_general(aggregate, grad_pre_b, TN, preferred_element_type=F32)
    column = jnp.sum(grad_pre, axis=0, keepdims=True)
    row_id = lax.broadcasted_iota(jnp.int32, (8, 128), 0)
    bias_tile = split(jnp.where(row_id == 0, column[:, :128], jnp.where(row_id == 1, column[:, 128:], 0.0)))

    @pl.loop(0, 32)
    def _(q):
        part = W[pl.ds(pl.multiple_of(q * 16, 16), 16), :].astype(BF)
        a, b = lax.div(q, 16), lax.rem(q, 16)
        u, v = lax.div(b, 4), lax.rem(b, 4)
        M[a, u, v, 0] = part[:, 0:128]
        M[a, u, v, 1] = part[:, 128:256]
        M[a, u, v, 2] = bias_tile

    wc().start()
    gfeat_own = lax.dot_general(grad_pre_b, w_self[...], NT, preferred_element_type=F32)
    wc().wait_recv()
    keep(M1, wide(M[c]) + wide(MC[...]))
    each3(lambda d: wx(d).start())

    each3(lambda d: wx(d).wait_recv())
    keep(M2, wide(M1[x]) + wide(MX[0]) + wide(MX[1]) + wide(MX[2]))
    each3(lambda d: wy(d).start())

    @pl.loop(0, 4)
    def _(g):
        for k in range(2):

            @pl.when(g == k)
            def _():
                z5(k).wait_recv()
                z5(2 + k).start()

        @pl.when(g == 2)
        def _():
            z5(2).wait_recv()
            z5(3).wait_recv()

        @pl.when(g < 3)
        def _():
            each3(lambda d: y5(g + 1, d).start())

        @pl.when(g == 1)
        def _():
            each3(lambda d: wy(d).wait_recv())
            keep(M3, wide(M2[y]) + wide(MY[0]) + wide(MY[1]) + wide(MY[2]))
            each3(lambda d: wl(d).start())

        @pl.when(g == 2)
        def _():
            each3(lambda d: wl(d).wait_recv())
            keep(M4, (wide(M3[...]) + wide(ML[0])) + (wide(ML[1]) + wide(ML[2])))
            wh(0).start()
            wh(1).start()

        @pl.when(g == 3)
        def _():
            wh(0).wait_recv()
            wh(2).start()

        each3(lambda d: y5(g, d).wait_recv())
        c5(g).start()
        c5(g).wait_recv()
        zq = mod4(zh + 4 - z_near(g))
        chunk = pl.ds(pl.multiple_of(zq * 1024, 1024), 1024)

        @pl.loop(0, 4)
        def _(n):
            part = xor4(zl, 3 - n)
            columns = pl.ds(pl.multiple_of(part * 512, 512), 512)
            ACC[part] += lax.dot_general(
                A[chunk, columns], G[zq].reshape(1024, 256), TN, preferred_element_type=F32
            )

            @pl.when(g == 3)
            def _():
                BP[part] = ACC[part].astype(BF).reshape(4, 128, 256)

            @pl.when((g == 3) & (n < 2))
            def _():
                each3(lambda d: x6(n, d).start())

    wh(1).wait_recv()
    wh(2).wait_recv()
    sums = (wide(M4[...]) + wide(MH[2])) + (wide(MH[0]) + wide(MH[1]))
    R[c, y, x] = sums[0:2].astype(BF)
    each3(lambda d: vx(d).start())
    each3(lambda d: x6(2, d).start())
    each3(lambda d: x6(3, d).start())

    @pl.loop(0, 4)
    def _(n):
        each3(lambda d: x6(n, d).wait_recv())
        part_sum = BP[xor4(zl, 3 - n), x].astype(F32)
        for d in range(3):
            part_sum = part_sum + XR[n, d].astype(F32)
        TOT[...] = part_sum

        @pl.when(n < 3)
        def _():
            XS[n] = part_sum.astype(BF)
            l6(n).start()

        @pl.when(n == 1)
        def _():
            each3(lambda d: vx(d).wait_recv())
            each3(lambda d: vy(d).start())

    factor = 1.0 / 256.0
    bias_sum = joined(sums[2])
    gbias[...] = jnp.concatenate([bias_sum[0:1], bias_sum[1:2]], axis=1) * factor
    each3(lambda d: vy(d).wait_recv())
    vc().start()

    def assemble(a):
        @pl.loop(0, 16)
        def _(q):
            u, v = lax.div(q, 4), lax.rem(q, 4)
            rows = pl.ds(pl.multiple_of(a * 256 + q * 16, 16), 16)
            W[rows, :] = wide(jnp.concatenate([R[a, v, u, 0], R[a, v, u, 1]], axis=1)) * factor

    assemble(c)
    total = TOT[...] + gfeat_own
    for n in range(3):
        l6(n).wait_recv()
        total = total + LR[n].astype(F32)
    gfeat[...] = total.astype(BF)
    vc().wait_recv()
    assemble(oc)
    saves = [
        pltpu.make_async_copy(gfeat, gfeat_h, osem.at[1]),
        pltpu.make_async_copy(W.at[pl.ds(0, 256)], gself_h, osem.at[2]),
        pltpu.make_async_copy(W.at[pl.ds(256, 256)], gneigh_h, osem.at[3]),
        pltpu.make_async_copy(gbias, gbias_h, osem.at[4]),
    ]
    for save in saves:
        save.start()

    @pl.loop(0, 4)
    def _(n):
        c3(n).wait_send()
        c5(n).wait_send()

        @each3
        def _(d):
            x1(n, d).wait_send()
            y3(n, d).wait_send()
            y5(n, d).wait_send()
            x6(n, d).wait_send()

    @each3
    def _(d):
        for copy in (z1(d), l6(d - 1), wx(d), wy(d), wl(d), vy(d), vx(d)):
            copy.wait_send()

    for copy in (wc(), vc(), wh(0), wh(1), wh(2), *map(z3, range(4)), *map(z5, range(4))):
        copy.wait_send()
    save_out.wait()
    for save in saves:
        save.wait()


def hand_over(*refs):
    n = len(refs) // 2
    for k in range(n):
        refs[n + k][...] = refs[k][...]


def body(features, adj_tiles, tile_row, tile_col, tile_count, w_self, w_neigh, bias_vec, cotangent):
    vmem = pl.BlockSpec(memory_space=pltpu.VMEM)
    whole = pl.BlockSpec(memory_space=pl.ANY)
    dma = pltpu.SemaphoreType.DMA
    sds = jax.ShapeDtypeStruct
    results = (
        sds((128, 256), BF), sds((128, 256), BF), sds((256, 256), F32), sds((256, 256), F32), sds((1, 256), F32),
    )
    held = pl.pallas_call(
        kernel,
        out_shape=results,
        in_specs=[whole] * 9,
        out_specs=(whole,) * 5,
        scratch_shapes=[
            pltpu.VMEM((4096, 2048), BF),
            pltpu.VMEM((SLOTS + 1, 128, 128), BF),
            pltpu.VMEM((16, 128, 256), BF),
            pltpu.VMEM((4, 2, 4, 128, 256), BF),
            pltpu.VMEM((4, 4, 128, 256), BF),
            pltpu.VMEM((4, 4, 128, 256), BF),
            pltpu.VMEM((4, 3, 128, 256), BF),
            pltpu.VMEM((3, 128, 256), BF),
            pltpu.VMEM((3, 128, 256), BF),
            pltpu.VMEM((128, 256), F32),
            pltpu.VMEM((4, 2, 4, 128, 256), BF),
            pltpu.VMEM((4, 512, 256), F32),
            pltpu.VMEM((4, 4, 128, 256), BF),
            pltpu.VMEM((4, 3, 128, 256), BF),
            pltpu.VMEM((3, 128, 256), BF),
            pltpu.VMEM((3, 128, 256), BF),
            pltpu.VMEM((512, 256), F32),
            pltpu.VMEM((2, 4, 4, 3, 16, 128), BF),
            pltpu.VMEM((4, 4, 3, 16, 128), BF),
            pltpu.VMEM((4, 4, 3, 16, 128), BF),
            pltpu.VMEM((3, 4, 3, 16, 128), BF),
            pltpu.VMEM((4, 3, 16, 128), BF),
            pltpu.VMEM((3, 3, 16, 128), BF),
            pltpu.VMEM((3, 16, 128), BF),
            pltpu.VMEM((3, 3, 16, 128), BF),
            pltpu.VMEM((3, 16, 128), BF),
            pltpu.VMEM((3, 3, 16, 128), BF),
            pltpu.VMEM((2, 4, 4, 2, 16, 128), BF),
            pltpu.VMEM((256, 256), BF),
            pltpu.VMEM((256, 256), BF),
            pltpu.VMEM((1, 256), F32),
            pltpu.VMEM((128, 256), BF),
            pltpu.VMEM((128, 256), BF),
            pltpu.VMEM((128, 256), BF),
            pltpu.VMEM((1, 256), F32),
            pltpu.SMEM((1, 1, SLOTS), jnp.int32),
            pltpu.SMEM((1, 1, SLOTS), jnp.int32),
            pltpu.SMEM((1, 1), jnp.int32),
            pltpu.VMEM((8, 128), jnp.int32),
            pltpu.SMEM((8, 128), jnp.int32),
            dma((10,)), dma((5,)),
            dma((3,)), dma((3,)), dma((4, 3)), dma((4, 3)),
            dma((4,)), dma((4,)), dma((4, 3)), dma((4, 3)), dma((4,)), dma((4,)),
            dma((4,)), dma((4,)), dma((4, 3)), dma((4, 3)), dma((4,)), dma((4,)),
            dma((4, 3)), dma((4, 3)), dma((3,)), dma((3,)),
            dma((21,)), dma((21,)),
        ],
        compiler_params=pltpu.CompilerParams(
            collective_id=0, has_side_effects=True, vmem_limit_bytes=60 * 2**20
        ),
    )(
        tile_row, tile_col, tile_count, features, adj_tiles, w_self, w_neigh, bias_vec.reshape(1, 256), cotangent
    )
    out, gfeat, gself, gneigh, gbias = pl.pallas_call(
        hand_over,
        out_shape=results,
        in_specs=[vmem] * 5,
        out_specs=(vmem,) * 5,
    )(*held)
    return out, gfeat, gself, gneigh, gbias.reshape(256)


def solution(mesh):
    placed = (
        P(("row", "col"), None),
        P("row", "col", None, None, None),
        P("row", "col", None),
        P("row", "col", None),
        P("row", "col"),
        P(),
        P(),
        P(),
        P(("row", "col"), None),
    )
    return jax.shard_map(
        body,
        mesh=mesh,
        in_specs=placed,
        out_specs=(P(("row", "col"), None), P(("row", "col"), None), P(), P(), P()),
        check_vma=False,
    )
```

```python
import jax
import jax.numpy as jnp
from jax import lax
from jax.experimental import pallas as pl
from jax.experimental.pallas import tpu as pltpu
from jax.sharding import PartitionSpec as P

MESH = pl.DeviceIdType.MESH
BF = jnp.bfloat16
F32 = jnp.float32
SLOTS = 96
ZERO = SLOTS
TN = (((0,), (0,)), ((), ()))
NT = (((1,), (1,)), ((), ()))


def mod4(v):
    return lax.rem(v, 4)


def xor4(v, d):
    v0, v1, d0, d1 = lax.rem(v, 2), lax.div(v, 2), d % 2, d // 2
    return 2 * (v1 + d1 - 2 * v1 * d1) + v0 + d0 - 2 * v0 * d0


def z_far(n):
    return mod4(2 - n + 3 * lax.div(n * (n - 1), 2))


def z_near(n):
    return mod4(n + lax.div(n * (n - 1), 2))


def dot(a, b):
    return jnp.dot(a, b, preferred_element_type=F32)


def kernel(
    rows_h, cols_h, count_h, feat_h, tiles_h, w_self_h, w_neigh_h, bias_h, cot_h,
    out_h, gfeat_h, weights_h, gbias_h,
    A, T, X, PA, CR, Y, YR, ZS, ZR, TOT, G, ACC, BP, XR, XS, LR,
    LEFT, W, M, MC, M1, MX, M2, MY, M3, ML, M4, MH, R,
    w_self, w_neigh, bias, cot, out, gfeat, gbias, rows_in, cols_in, count_in, table, inv,
    lsem, osem, s1z, r1z, s1x, r1x, s3c, r3c, s3y, r3y, s3z, r3z,
    s5z, r5z, s5y, r5y, s5c, r5c, s6x, r6x, s6l, r6l, sw, rw,
):
    i = lax.axis_index("row")
    j = lax.axis_index("col")
    zl, x = lax.div(i, 4), lax.rem(i, 4)
    zh, yc = lax.div(j, 8), lax.rem(j, 8)
    y, c = lax.div(yc, 2), lax.rem(yc, 2)
    oc = 1 - c

    def dev(zl_=zl, x_=x, zh_=zh, y_=y, c_=c):
        return (zl_ * 4 + x_, zh_ * 8 + y_ * 2 + c_)

    def to_x(d):
        return dev(x_=mod4(x + d))

    def to_y(d):
        return dev(y_=mod4(y + d))

    def to_zh(d):
        return dev(zh_=mod4(zh + d))

    def to_zl(d):
        return dev(zl_=xor4(zl, d))

    def remote(src, dst, ssem, rsem, device):
        return pltpu.make_async_remote_copy(
            src_ref=src, dst_ref=dst, send_sem=ssem, recv_sem=rsem, device_id=device, device_id_type=MESH
        )

    def each3(act):
        pl.loop(1, 4)(lambda k: act(1 + lax.rem(k, 3)))

    def z1(d):
        return remote(X.at[i], X.at[i], s1z.at[d - 1], r1z.at[d - 1], to_zl(d))

    def x1(d, e):
        block = X.at[xor4(zl, d) * 4 + x]
        return remote(block, block, s1x.at[d, e - 1], r1x.at[d, e - 1], to_x(e))

    def c3(n):
        return remote(PA.at[mod4(zh + z_far(n)), oc], CR.at[n], s3c.at[n], r3c.at[n], dev(c_=oc))

    def y3(n, d):
        share = Y.at[mod4(zh + z_far(n)), mod4(y + d)]
        return remote(share, YR.at[n, d - 1], s3y.at[n, d - 1], r3y.at[n, d - 1], to_y(d))

    def half(ref, k):
        return ref.at[pl.ds(64 * k, 64)]

    def z3(n):
        src = half(ZS.at[0], n) if n < 2 else ZS.at[n - 1]
        dst = half(ZR.at[0], n) if n < 2 else ZR.at[n - 1]
        return remote(src, dst, s3z.at[n], r3z.at[n], to_zh(1 + 2 * (n % 2)))

    def z5(k):
        if k in (2, 3):
            block = G.at[mod4(zh + 3 - 2 * (k % 2)), c, y]
        else:
            block = G.at[zh, c, y]
        block = half(block, (k + k // 4) % 2)
        return remote(block, block, s5z.at[k], r5z.at[k], to_zh(1 + 2 * (k % 2)))

    def y5(g, d):
        block = G.at[mod4(zh + 4 - z_near(g)), c, y]
        return remote(block, block, s5y.at[g, d - 1], r5y.at[g, d - 1], to_y(d))

    def c5(g):
        slab = G.at[mod4(zh + 4 - z_near(g)), c]
        return remote(slab, slab, s5c.at[g], r5c.at[g], dev(c_=oc))

    def x6(n, d):
        share = BP.at[xor4(zl, 3 - n), mod4(x + d)]
        return remote(share, XR.at[n, d - 1], s6x.at[n, d - 1], r6x.at[n, d - 1], to_x(d))

    def l6(n):
        return remote(XS.at[n], LR.at[n], s6l.at[n], r6l.at[n], to_zl(3 - n))

    def w(k, src, dst, device):
        return remote(src, dst, sw.at[k], rw.at[k], device)

    def wc():
        return w(0, M.at[oc], MC, dev(c_=oc))

    def wx(d):
        return w(d, M1.at[mod4(x + d)], MX.at[d - 1], to_x(d))

    def wy(d):
        return w(3 + d, M2.at[mod4(y + d)], MY.at[d - 1], to_y(d))

    def wl(d):
        return w(6 + d, M3, ML.at[d - 1], to_zl(d))

    def wh(k):
        return w(20 if k == 2 else 10 + k, MH.at[0] if k == 2 else M4, MH.at[k], to_zh(1 + 2 * (k % 2)))

    def vx(d):
        return w(12 + d, R.at[c, y, x], R.at[c, y, x], to_x(d))

    def vy(d):
        return w(15 + d, R.at[c, y], R.at[c, y], to_y(d))

    def vc():
        return w(19, R.at[c], R.at[c], dev(c_=oc))

    barrier = pltpu.get_barrier_semaphore()

    def greet(device):
        pl.semaphore_signal(barrier, inc=1, device_id=device, device_id_type=MESH)

    @each3
    def _(d):
        greet(to_zl(d))
        greet(to_x(d))
        greet(to_y(d))

    greet(dev(c_=oc))
    greet(to_zh(1))
    greet(to_zh(3))

    loads = [
        pltpu.make_async_copy(feat_h, X.at[i], lsem.at[0]),
        pltpu.make_async_copy(tiles_h.at[0, 0], T.at[pl.ds(0, SLOTS)], lsem.at[1]),
        pltpu.make_async_copy(w_self_h, w_self, lsem.at[2]),
        pltpu.make_async_copy(w_neigh_h, w_neigh, lsem.at[3]),
        pltpu.make_async_copy(cot_h, cot, lsem.at[4]),
        pltpu.make_async_copy(bias_h, bias, lsem.at[5]),
        pltpu.make_async_copy(rows_h, rows_in, lsem.at[6]),
        pltpu.make_async_copy(cols_h, cols_in, lsem.at[7]),
        pltpu.make_async_copy(count_h, count_in, lsem.at[8]),
    ]
    for load in loads:
        load.start()

    for load in loads[6:]:
        load.wait()
    place_id = lax.broadcasted_iota(jnp.int32, (8, 128), 0) * 128 + lax.broadcasted_iota(jnp.int32, (8, 128), 1)
    count = count_in[0, 0]

    def note(t, found):
        r = rows_in[0, 0, t]
        place = lax.div(r, 8) * 8 + lax.rem(r, 2) * 4 + lax.div(lax.rem(r, 8), 2)
        place = jnp.where(t < count, place * 16 + cols_in[0, 0, t], -1)
        return jnp.where(place_id == place, t, found)

    table[...] = lax.fori_loop(0, SLOTS, note, jnp.full((8, 128), ZERO, jnp.int32))
    to_smem = pltpu.make_async_copy(table, inv, lsem.at[9])
    to_smem.start()
    T[ZERO] = jnp.zeros((128, 128), BF)
    ACC[...] = jnp.zeros_like(ACC)
    loads[0].wait()
    pl.semaphore_wait(barrier, 12)

    pl.loop(0, 3)(lambda k: z1(3 - k).start())
    each3(lambda d: x1(0, d).start())
    to_smem.wait()
    for load in loads[1:6]:
        load.wait()

    @pl.loop(0, 4)
    def _(n):
        @pl.when(n > 0)
        def _():
            z1(4 - n).wait_recv()
            each3(lambda e: x1(4 - n, e).start())

        @pl.loop(n * 8, n * 8 + 8)
        def _(p):
            tile_rows = pl.ds(pl.multiple_of(p * 128, 128), 128)
            for q in range(16):
                A[tile_rows, q * 128 : (q + 1) * 128] = T[inv[lax.div(p, 8), lax.rem(p, 8) * 16 + q]]

    own_term = dot(X[i], w_self[...]) + bias[...]

    @pl.loop(0, 4)
    def _(d):
        each3(lambda e: x1(d, e).wait_recv())

    @pl.loop(0, 5)
    def _(n):
        @pl.when(n < 4)
        def _():
            zq = mod4(zh + z_far(n))
            chunk = pl.ds(pl.multiple_of(zq * 1024, 1024), 1024)
            PA[zq] = dot(A[chunk, :], X[...].reshape(2048, 256)).astype(BF).reshape(2, 4, 128, 256)
            c3(n).start()

        @pl.when(n > 0)
        def _():
            zq = mod4(zh + z_far(n - 1))
            c3(n - 1).wait_recv()
            Y[zq] = (PA[zq, c].astype(F32) + CR[n - 1].astype(F32)).astype(BF)
            each3(lambda d: y3(n - 1, d).start())

    @pl.loop(0, 4)
    def _(n):
        each3(lambda d: y3(n, d).wait_recv())
        total = Y[mod4(zh + z_far(n)), y].astype(F32)
        for d in range(3):
            total = total + YR[n, d].astype(F32)
        TOT[...] = total

        @pl.when(n == 0)
        def _():
            ZS[0] = total.astype(BF)
            z3(0).start()
            z3(1).start()

        for k in range(2):

            @pl.when(n == 1 + k)
            def _():
                z3(k).wait_recv()
                near = slice(64 * k, 64 * k + 64)
                TOT[near] += ZR[0, near].astype(F32)
                ZS[1 + k] = TOT[...].astype(BF)
                z3(2 + k).start()

    z3(2).wait_recv()
    z3(3).wait_recv()
    total = TOT[...] + ZR[1].astype(F32) + ZR[2].astype(F32)
    aggregate = total.astype(BF)

    preact = own_term + dot(aggregate, w_neigh[...])
    sigma = jax.nn.sigmoid(preact)
    grad_pre = cot[...].astype(F32) * sigma * (1.0 + preact * (1.0 - sigma))
    grad_pre_b = grad_pre.astype(BF)
    G[zh, c, y] = lax.dot_general(grad_pre_b, w_neigh[...], NT, preferred_element_type=F32).astype(BF)

    for k in (0, 1, 4, 5):
        z5(k).start()
    each3(lambda d: y5(0, d).start())
    def split(value):
        high = value.astype(BF).astype(F32)
        return jnp.concatenate([high, value - high], axis=0).astype(BF)

    def joined(tile):
        return tile[0:8] + tile[8:16]

    def keep(ref, total):
        ref[...] = total.astype(BF)
        lead = total.ndim - 3
        tile = split(joined(total[(0,) * lead + (2,)]))
        ref[(slice(None),) * lead + (2,)] = jnp.broadcast_to(tile, total.shape[:lead] + tile.shape)

    def wide(value):
        return value.astype(F32)

    LEFT[0] = X[i]
    LEFT[1] = aggregate
    column = jnp.sum(grad_pre, axis=0, keepdims=True)
    row_id = lax.broadcasted_iota(jnp.int32, (8, 128), 0)
    bias_tile = split(jnp.where(row_id == 0, column[:, :128], jnp.where(row_id == 1, column[:, 128:], 0.0)))

    @pl.loop(0, 2)
    def _(k):
        a = lax.rem(oc + k, 2)
        W[0:256] = lax.dot_general(LEFT[a], grad_pre_b, TN, preferred_element_type=F32)

        @pl.loop(0, 4)
        def _(u):
            for v in range(4):
                part = W[pl.ds(pl.multiple_of(u * 64 + v * 16, 16), 16), :].astype(BF)
                M[a, u, v, 0] = part[:, 0:128]
                M[a, u, v, 1] = part[:, 128:256]
                M[a, u, v, 2] = bias_tile

        @pl.when(k == 0)
        def _():
            wc().start()

    wc().wait_recv()
    keep(M1, wide(M[c]) + wide(MC[...]))
    each3(lambda d: wx(d).start())
    out[...] = (preact * sigma).astype(BF)
    save_out = pltpu.make_async_copy(out, out_h, osem.at[0])
    save_out.start()
    gfeat_own = lax.dot_general(grad_pre_b, w_self[...], NT, preferred_element_type=F32)

    each3(lambda d: wx(d).wait_recv())
    keep(M2, wide(M1[x]) + wide(MX[0]) + wide(MX[1]) + wide(MX[2]))
    each3(lambda d: wy(d).start())

    @pl.loop(0, 4)
    def _(g):
        @pl.when(g == 0)
        def _():
            for k in range(2):
                z5(k).wait_recv()
                z5(2 + k).start()
            z5(4).wait_recv()

        @pl.when(g == 1)
        def _():
            z5(5).wait_recv()

        @pl.when(g == 2)
        def _():
            z5(2).wait_recv()
            z5(3).wait_recv()

        @pl.when(g < 3)
        def _():
            each3(lambda d: y5(g + 1, d).start())

        @pl.when(g == 1)
        def _():
            each3(lambda d: wy(d).wait_recv())
            keep(M3, wide(M2[y]) + wide(MY[0]) + wide(MY[1]) + wide(MY[2]))
            each3(lambda d: wl(d).start())

        @pl.when(g == 2)
        def _():
            each3(lambda d: wl(d).wait_recv())
            keep(M4, (wide(M3[...]) + wide(ML[0])) + (wide(ML[1]) + wide(ML[2])))
            wh(0).start()
            wh(1).start()

        @pl.when(g == 3)
        def _():
            wh(0).wait_recv()
            wh(2).start()

        each3(lambda d: y5(g, d).wait_recv())
        c5(g).start()
        c5(g).wait_recv()
        zq = mod4(zh + 4 - z_near(g))
        chunk = pl.ds(pl.multiple_of(zq * 1024, 1024), 1024)

        @pl.loop(0, 4)
        def _(n):
            part = xor4(zl, 3 - n)
            columns = pl.ds(pl.multiple_of(part * 512, 512), 512)
            ACC[part] += lax.dot_general(
                A[chunk, columns], G[zq].reshape(1024, 256), TN, preferred_element_type=F32
            )

            @pl.when(g == 3)
            def _():
                BP[part] = ACC[part].astype(BF).reshape(4, 128, 256)

            @pl.when((g == 3) & (n < 2))
            def _():
                each3(lambda d: x6(n, d).start())

    wh(1).wait_recv()
    wh(2).wait_recv()
    sums = (wide(M4[...]) + wide(MH[2])) + (wide(MH[0]) + wide(MH[1]))
    R[c, y, x] = sums[0:2].astype(BF)
    each3(lambda d: vx(d).start())
    each3(lambda d: x6(2, d).start())
    each3(lambda d: x6(3, d).start())

    @pl.loop(0, 4)
    def _(n):
        each3(lambda d: x6(n, d).wait_recv())
        part_sum = BP[xor4(zl, 3 - n), x].astype(F32)
        for d in range(3):
            part_sum = part_sum + XR[n, d].astype(F32)
        TOT[...] = part_sum

        @pl.when(n < 3)
        def _():
            XS[n] = part_sum.astype(BF)
            l6(n).start()

        @pl.when(n == 1)
        def _():
            each3(lambda d: vx(d).wait_recv())
            each3(lambda d: vy(d).start())

    factor = 1.0 / 256.0
    bias_sum = joined(sums[2])
    gbias[...] = jnp.concatenate([bias_sum[0:1], bias_sum[1:2]], axis=1) * factor
    each3(lambda d: vy(d).wait_recv())
    vc().start()

    def save_weights(a):
        @pl.loop(0, 4)
        def _(u):
            for v in range(4):
                rows = pl.ds(pl.multiple_of(a * 256 + u * 64 + v * 16, 16), 16)
                W[rows, :] = wide(jnp.concatenate([R[a, v, u, 0], R[a, v, u, 1]], axis=1)) * factor

        return pltpu.make_async_copy(
            W.at[pl.ds(pl.multiple_of(a * 256, 256), 256)], weights_h.at[pl.ds(pl.multiple_of(a * 256, 256), 256)],
            osem.at[2 + a],
        )

    save_own = save_weights(c)
    save_own.start()
    total = TOT[...] + gfeat_own
    for n in range(3):
        l6(n).wait_recv()
        total = total + LR[n].astype(F32)
    gfeat[...] = total.astype(BF)
    save_gfeat = pltpu.make_async_copy(gfeat, gfeat_h, osem.at[1])
    save_gfeat.start()
    save_bias = pltpu.make_async_copy(gbias, gbias_h, osem.at[4])
    save_bias.start()
    vc().wait_recv()
    save_other = save_weights(oc)
    save_other.start()
    saves = [save_own, save_gfeat, save_bias, save_other]

    @pl.loop(0, 4)
    def _(n):
        c3(n).wait_send()
        c5(n).wait_send()

        @each3
        def _(d):
            x1(n, d).wait_send()
            y3(n, d).wait_send()
            y5(n, d).wait_send()
            x6(n, d).wait_send()

    @each3
    def _(d):
        for copy in (z1(d), l6(d - 1), wx(d), wy(d), wl(d), vy(d), vx(d)):
            copy.wait_send()

    for copy in (wc(), vc(), wh(0), wh(1), wh(2), *map(z3, range(4)), *map(z5, range(6))):
        copy.wait_send()
    save_out.wait()
    for save in saves:
        save.wait()


def hand_over(out, gfeat, weights, gbias, out_to, gfeat_to, gself_to, gneigh_to, gbias_to):
    out_to[...] = out[...]
    gfeat_to[...] = gfeat[...]
    gself_to[...] = weights[0:256]
    gneigh_to[...] = weights[256:512]
    gbias_to[...] = gbias[...]


def body(features, adj_tiles, tile_row, tile_col, tile_count, w_self, w_neigh, bias_vec, cotangent):
    vmem = pl.BlockSpec(memory_space=pltpu.VMEM)
    whole = pl.BlockSpec(memory_space=pl.ANY)
    dma = pltpu.SemaphoreType.DMA
    sds = jax.ShapeDtypeStruct
    results = (
        sds((128, 256), BF), sds((128, 256), BF), sds((256, 256), F32), sds((256, 256), F32), sds((1, 256), F32),
    )
    held = pl.pallas_call(
        kernel,
        out_shape=(results[0], results[1], sds((512, 256), F32), results[4]),
        in_specs=[whole] * 9,
        out_specs=(whole,) * 4,
        scratch_shapes=[
            pltpu.VMEM((4096, 2048), BF),
            pltpu.VMEM((SLOTS + 1, 128, 128), BF),
            pltpu.VMEM((16, 128, 256), BF),
            pltpu.VMEM((4, 2, 4, 128, 256), BF),
            pltpu.VMEM((4, 4, 128, 256), BF),
            pltpu.VMEM((4, 4, 128, 256), BF),
            pltpu.VMEM((4, 3, 128, 256), BF),
            pltpu.VMEM((3, 128, 256), BF),
            pltpu.VMEM((3, 128, 256), BF),
            pltpu.VMEM((128, 256), F32),
            pltpu.VMEM((4, 2, 4, 128, 256), BF),
            pltpu.VMEM((4, 512, 256), F32),
            pltpu.VMEM((4, 4, 128, 256), BF),
            pltpu.VMEM((4, 3, 128, 256), BF),
            pltpu.VMEM((3, 128, 256), BF),
            pltpu.VMEM((3, 128, 256), BF),
            pltpu.VMEM((2, 128, 256), BF),
            pltpu.VMEM((512, 256), F32),
            pltpu.VMEM((2, 4, 4, 3, 16, 128), BF),
            pltpu.VMEM((4, 4, 3, 16, 128), BF),
            pltpu.VMEM((4, 4, 3, 16, 128), BF),
            pltpu.VMEM((3, 4, 3, 16, 128), BF),
            pltpu.VMEM((4, 3, 16, 128), BF),
            pltpu.VMEM((3, 3, 16, 128), BF),
            pltpu.VMEM((3, 16, 128), BF),
            pltpu.VMEM((3, 3, 16, 128), BF),
            pltpu.VMEM((3, 16, 128), BF),
            pltpu.VMEM((3, 3, 16, 128), BF),
            pltpu.VMEM((2, 4, 4, 2, 16, 128), BF),
            pltpu.VMEM((256, 256), BF),
            pltpu.VMEM((256, 256), BF),
            pltpu.VMEM((1, 256), F32),
            pltpu.VMEM((128, 256), BF),
            pltpu.VMEM((128, 256), BF),
            pltpu.VMEM((128, 256), BF),
            pltpu.VMEM((1, 256), F32),
            pltpu.SMEM((1, 1, SLOTS), jnp.int32),
            pltpu.SMEM((1, 1, SLOTS), jnp.int32),
            pltpu.SMEM((1, 1), jnp.int32),
            pltpu.VMEM((8, 128), jnp.int32),
            pltpu.SMEM((8, 128), jnp.int32),
            dma((10,)), dma((5,)),
            dma((3,)), dma((3,)), dma((4, 3)), dma((4, 3)),
            dma((4,)), dma((4,)), dma((4, 3)), dma((4, 3)), dma((4,)), dma((4,)),
            dma((6,)), dma((6,)), dma((4, 3)), dma((4, 3)), dma((4,)), dma((4,)),
            dma((4, 3)), dma((4, 3)), dma((3,)), dma((3,)),
            dma((21,)), dma((21,)),
        ],
        compiler_params=pltpu.CompilerParams(
            collective_id=0, has_side_effects=True, vmem_limit_bytes=60 * 2**20
        ),
    )(
        tile_row, tile_col, tile_count, features, adj_tiles, w_self, w_neigh, bias_vec.reshape(1, 256), cotangent
    )
    out, gfeat, gself, gneigh, gbias = pl.pallas_call(
        hand_over,
        out_shape=results,
        in_specs=[vmem] * 4,
        out_specs=(vmem,) * 5,
    )(*held)
    return out, gfeat, gself, gneigh, gbias.reshape(256)


def solution(mesh):
    placed = (
        P(("row", "col"), None),
        P("row", "col", None, None, None),
        P("row", "col", None),
        P("row", "col", None),
        P("row", "col"),
        P(),
        P(),
        P(),
        P(("row", "col"), None),
    )
    return jax.shard_map(
        body,
        mesh=mesh,
        in_specs=placed,
        out_specs=(P(("row", "col"), None), P(("row", "col"), None), P(), P(), P()),
        check_vma=False,
    )
```
